32 devices in a mesh: slab: 8 (over y, x, core), sub: 4 (over z).
Axes of the slice: x: 2, y: 2, z: 4, core: 2. Of those that a mesh axis runs over, the one named last changes fastest.
Arguments:
- density: float32 [2, 32, 16, 2, 296], P(None, 'slab', 'sub'), may hold values from -6 to 6
- occupied: int32 [32, 16, 2], P('slab', 'sub'), may hold values 0 or 1
- kernels: float32 [2, 316, 4096], P(None, None, ('slab', 'sub')), may hold values from -6 to 6
Outputs:
- check_potential: float32 [2, 32, 16, 2, 296], P(None, 'slab', 'sub')
The draws below stay inside these ranges and needn't reach their ends.
All inputs are finite; a program needn't handle non-finite values. No bound on the sum of `occupied` on one device may be relied on, other than what follows from the above.
Results may differ from the reference program's by a relative error of at most 0.000071.
Values sent between devices are 32-bit elements; how exact they have to be, the bound alone decides.
No kernel may reach another device: no remote copies, remote signals or barrier semaphores. Data moves between devices by JAX's collectives and lax.ppermute only.
A program may use at most 128 MiB of HBM per device.

```python
import jax
import jax.numpy as jnp
import numpy as np
from jax import lax

P_SIZE = 8
G = 16
F = 4096
SURF = 296
OFFS = 316
NZB = 2
NXB = 32
NYB = 16


def plant(entries, rng, least, top_value):
    spot = [jax.random.randint(jax.random.fold_in(rng, axis), (), 0, length) for axis, length in enumerate(entries.shape)]
    longest = entries.shape.index(max(entries.shape))
    neighbour = spot[:longest] + [(spot[longest] + 1) % entries.shape[longest]] + spot[longest + 1:]
    return entries.at[tuple(spot)].set(least).at[tuple(neighbour)].set(top_value)


def block_levels(own_key, dims, pieces, low, high):
    factor_of, own = 1.0, jax.random.fold_in(own_key, 6)
    for dim, blocks in pieces:
        heights = jnp.exp(jax.random.uniform(jax.random.fold_in(own, dim), (blocks,), jnp.float32, low / len(pieces), high / len(pieces)))
        factor_of = factor_of * jnp.repeat(heights, dims[dim] // blocks).reshape([-1 if axis == dim else 1 for axis in range(len(dims))])
    return factor_of


def noise(own_key, extent, spread, limit, shards=(), kind=jnp.bfloat16):
    values = spread * jax.random.normal(own_key, extent, jnp.float32)
    if shards:
        values = values * block_levels(own_key, extent, shards, -0.22, 0.18)
    return jnp.clip(values, -limit, limit).astype(kind)


def setup_inputs(seed: int = 0) -> dict:
    key_of = jax.random.split(jax.random.key(seed), 4)
    return {
        "density": noise(key_of[0], (2, NXB, NYB, NZB, SURF), 1.0, 6.0, ((1, 8), (2, 4)), jnp.float32),
        "occupied": plant((jax.random.randint(key_of[1], (NXB, NYB, NZB), 0, 5) < 3).astype(jnp.int32), jax.random.fold_in(key_of[1], 1), 0, 1),
        "kernels": noise(key_of[2], (2, OFFS, F), 0.4, 6.0, ((2, 32),), jnp.float32),
    }


def surface_points(edge_count):
    rows_found = []
    for first in range(edge_count):
        for second in range(edge_count):
            for third in range(edge_count):
                if min(first, second, third) == 0 or max(first, second, third) == edge_count - 1:
                    rows_found.append((first, second, third))
    return np.array(rows_found, dtype=np.int32).T


def offset_list():
    offsets = []
    for step_x in range(-3, 4):
        for step_y in range(-3, 4):
            for step_z in range(-3, 4):
                if max(abs(step_x), abs(step_y), abs(step_z)) > 1:
                    offsets.append((step_x, step_y, step_z))
    return offsets


def allowed(offset_step, parity):
    return (offset_step >= -2 - parity) & (offset_step <= 3 - parity)


def translate_block(block_pair):
    spectra_block, kernel_block = block_pair
    padded = jnp.pad(spectra_block, ((0, 0), (3, 3), (3, 3), (3, 3)))
    parity_x = np.arange(NXB) % 2
    parity_y = np.arange(NYB) % 2
    parity_z = np.arange(NZB) % 2
    summed = jnp.zeros_like(spectra_block)
    for kernel_slot, (step_x, step_y, step_z) in enumerate(offset_list()):
        usable = allowed(step_x, parity_x)[:, None, None] & allowed(step_y, parity_y)[None, :, None] & allowed(step_z, parity_z)[None, None, :]
        source = padded[:, 3 + step_x:3 + step_x + NXB, 3 + step_y:3 + step_y + NYB, 3 + step_z:3 + step_z + NZB]
        product = kernel_block[kernel_slot][:, None, None, None] * source
        summed = summed + jnp.where(jnp.asarray(usable)[None], product, 0.0)
    return summed


def reference(density, occupied, kernels):
    points = surface_points(P_SIZE)
    occupied_flag = occupied > 0
    masked = jnp.where(occupied_flag[None, :, :, :, None], density, 0.0)
    values = lax.complex(masked[0], masked[1])
    embedded = jnp.zeros((NXB, NYB, NZB, G, G, G), values.dtype)
    embedded = embedded.at[:, :, :, points[0], points[1], points[2]].set(values)
    spectra = jnp.fft.fftn(embedded, axes=(3, 4, 5)).reshape(NXB, NYB, NZB, F)
    blocks = jnp.moveaxis(spectra, 3, 0).reshape(F // 8, 8, NXB, NYB, NZB)
    kernel_values = lax.complex(kernels[0], kernels[1])
    kernel_blocks = jnp.moveaxis(kernel_values.reshape(OFFS, F // 8, 8), 1, 0)
    summed = lax.map(translate_block, (blocks, kernel_blocks))
    summed = jnp.moveaxis(summed.reshape(F, NXB, NYB, NZB), 0, 3).reshape(NXB, NYB, NZB, G, G, G)
    fields = jnp.fft.ifftn(summed, axes=(3, 4, 5))[:, :, :, points[0], points[1], points[2]]
    fields = jnp.where(occupied_flag[:, :, :, None], fields, 0.0)
    return jnp.stack([jnp.real(fields), jnp.imag(fields)]).astype(jnp.float32)
```

```python
import functools
import math

import jax
import jax.numpy as jnp
import numpy as np
from jax import lax
from jax.experimental import pallas as pl
from jax.experimental.pallas import tpu as pltpu
from jax.sharding import PartitionSpec as P

P_SIZE = 8
LANES = 128
VMEM_BYTES = 56 * 1024 * 1024
NEIGHBOURS = [(ex, ey) for ex in (-1, 0, 1) for ey in (-1, 0, 1) if (ex, ey) != (0, 0)]


def surface_points(edge_count):
    rows_found = []
    for first in range(edge_count):
        for second in range(edge_count):
            for third in range(edge_count):
                if min(first, second, third) == 0 or max(first, second, third) == edge_count - 1:
                    rows_found.append((first, second, third))
    return np.array(rows_found, dtype=np.int32).T


def column_groups():
    groups = {}
    slot = 0
    for step_x in range(-3, 4):
        for step_y in range(-3, 4):
            near = max(abs(step_x), abs(step_y)) <= 1
            if not near:
                groups[step_x, step_y] = slot + 2
            slot += 4 if near else 7
    return groups


GROUPS = column_groups()
GROUP_ROW = {key: 3 * place for place, key in enumerate(GROUPS)}
ROWS_KEPT = 3 * len(GROUPS)


def compact_body(kernel_ref, out_ref):
    for part in range(2):
        for key, first_slot in GROUPS.items():
            row = GROUP_ROW[key]
            out_ref[part, row:row + 3, :] = kernel_ref[part, first_slot:first_slot + 3, :]


def compact_kernels(kernels):
    return pl.pallas_call(
        compact_body,
        out_shape=jax.ShapeDtypeStruct((2, ROWS_KEPT, kernels.shape[-1]), jnp.float32),
        name="compact",
    )(kernels)


def prepare_body(kernel_ref, out_ref, raw_re, raw_im):
    raw_re[...] = jnp.zeros_like(raw_re)
    raw_im[...] = jnp.zeros_like(raw_im)
    for part, raw in enumerate((raw_re, raw_im)):
        for place, (ex, ey) in enumerate(NEIGHBOURS):
            for ax in range(3):
                for ay in range(3):
                    row = GROUP_ROW.get((2 * ex + ax - 1, 2 * ey + ay - 1))
                    if row is None:
                        continue
                    base = (ax * 3 + ay) * 3
                    for az in range(3):
                        at = (base + az) * 8 + place
                        raw[at:at + 1, :] = kernel_ref[0, part, row + az:row + az + 1, :]

    def transform(raw):
        values = np.empty((3, 3, 3), dtype=object)
        for ax in range(3):
            for ay in range(3):
                for az in range(3):
                    at = ((ax * 3 + ay) * 3 + az) * 8
                    values[ax, ay, az] = raw[at:at + 8, :]
        for axis in range(3):
            moved = np.moveaxis(values, axis, 0)
            fresh = np.empty((3, 3, 3), dtype=object)
            for first in range(3):
                for second in range(3):
                    low, mid, high = (moved[step, first, second] for step in range(3))
                    fresh[0, first, second] = low - mid
                    fresh[1, first, second] = high - mid
                    fresh[2, first, second] = mid
            values = np.moveaxis(fresh, 0, axis)
        return values

    real_part = transform(raw_re)
    imag_part = transform(raw_im)
    for cx in range(3):
        for cy in range(3):
            for cz in range(3):
                at = ((cx * 3 + cy) * 3 + cz) * 24
                k_re, k_im = real_part[cx, cy, cz], imag_part[cx, cy, cz]
                out_ref[0, at:at + 8, :] = k_re
                out_ref[0, at + 8:at + 16, :] = k_im - k_re
                out_ref[0, at + 16:at + 24, :] = k_re + k_im


def prepare_kernels(gathered):
    block_count = gathered.shape[0]
    return pl.pallas_call(
        prepare_body,
        grid=(block_count,),
        in_specs=[pl.BlockSpec((1, 2, ROWS_KEPT, LANES), lambda b: (b, 0, 0, 0))],
        out_specs=pl.BlockSpec((1, 27 * 24, LANES), lambda b: (b, 0, 0)),
        out_shape=jax.ShapeDtypeStruct((block_count, 27 * 24, LANES), jnp.float32),
        scratch_shapes=[pltpu.VMEM((27 * 8, LANES), jnp.float32)] * 2,
        name="prepare",
    )(gathered)


def split_bf16(values):
    high = values.astype(jnp.bfloat16)
    low = (values - high.astype(jnp.float32)).astype(jnp.bfloat16)
    return high, low


def translate_body(
    place_ref, c0, c1, c2, c3, inner_ref, outer_ref, w_high, w_low, kappa,
    o0, o1, o2, o3, rows_f32, a_high, a_low, spec_re, spec_im, comps, t_re, t_im, total,
):
    step = pl.program_id(0)
    sub, core = place_ref[0], place_ref[1]

    @pl.when(step == 0)
    def assemble():
        for k, chunk in enumerate((c0, c1, c2, c3)):
            source = sub ^ k
            for half in range(2):
                base = pl.multiple_of((2 * source + half) * 32, 32)
                rows_f32[pl.ds(base + 8, 16), :] = chunk[half * 16:half * 16 + 16, :]
                at = k * 16 + half * 8
                rows_f32[pl.ds(pl.multiple_of(base + 24 * (1 - core), 8), 8), :] = inner_ref[at:at + 8, :]
                rows_f32[pl.ds(pl.multiple_of(base + 24 * core, 8), 8), :] = outer_ref[at:at + 8, :]
        values = rows_f32[...]
        high, low = split_bf16(values)
        a_high[...] = high
        a_low[...] = low
        edge = jnp.zeros((32, LANES), jnp.float32)
        for spec in (spec_re, spec_im):
            spec[0:32, :] = edge
            spec[288:320, :] = edge
        total[...] = jnp.zeros_like(total)

    def dot(left, right):
        return jnp.dot(left, right, preferred_element_type=jnp.float32)

    def dot_nt(left, right):
        return lax.dot_general(
            left, right, (((1,), (1,)), ((), ())), preferred_element_type=jnp.float32
        )

    table_high, table_low = w_high[0], w_low[0]
    spectra = dot(a_high[...], table_high) + (dot(a_low[...], table_high) + dot(a_high[...], table_low))
    spec_re[32:288, :] = spectra[:, :LANES]
    spec_im[32:288, :] = spectra[:, LANES:]

    for ey in (-1, 0, 1):
        for parent in range(4):
            values = np.empty((2, 3, 3, 3), dtype=object)
            for part, spec in enumerate((spec_re, spec_im)):
                for px in range(2):
                    for py in range(2):
                        for pz in range(2):
                            row = (1 + ey) * 32 + (2 * parent + px) * 4 + pz * 2 + py
                            values[part, px, py, pz] = spec[pl.ds(row, 8, stride=32), :]
                for px in range(2):
                    for py in range(2):
                        values[part, px, py, 2] = values[part, px, py, 0] + values[part, px, py, 1]
                    for cz in range(3):
                        values[part, px, 2, cz] = values[part, px, 0, cz] + values[part, px, 1, cz]
                for cy in range(3):
                    for cz in range(3):
                        values[part, 2, cy, cz] = values[part, 0, cy, cz] + values[part, 1, cy, cz]
            for cx in range(3):
                for cy in range(3):
                    for cz in range(3):
                        comp = (cx * 3 + cy) * 3 + cz
                        at = (((ey + 1) * 4 + parent) * 27 + comp) * 24
                        s_re, s_im = values[0, cx, cy, cz], values[1, cx, cy, cz]
                        comps[at:at + 8, :] = s_re + s_im
                        comps[at + 8:at + 16, :] = s_re
                        comps[at + 16:at + 24, :] = s_im

    def product(cx, cy, cz):
        comp = (cx * 3 + cy) * 3 + cz
        sums = [[None] * 3 for _ in range(2)]
        for place, (ex, ey) in enumerate(NEIGHBOURS):
            for gauss in range(3):
                row = comp * 24 + gauss * 8 + place
                factor = jnp.broadcast_to(kappa[0, row:row + 1, :], (8, LANES))
                for parent in range(2):
                    at = (((ey + 1) * 4 + parent + 1 + ex) * 27 + comp) * 24 + gauss * 8
                    term = factor * comps[at:at + 8, :]
                    have = sums[parent][gauss]
                    sums[parent][gauss] = term if have is None else have + term
        found = []
        for parent in range(2):
            first, second, third = sums[parent]
            found += [first - third, first + second]
        return found

    def along_z(cx, cy):
        low, high, both = product(cx, cy, 0), product(cx, cy, 1), product(cx, cy, 2)
        return [b + h for b, h in zip(both, high)] + [b + l for b, l in zip(both, low)]

    def along_y(cx):
        low, high, both = along_z(cx, 0), along_z(cx, 1), along_z(cx, 2)
        return [b + h for b, h in zip(both, high)] + [b + l for b, l in zip(both, low)]

    low, high, both = along_y(0), along_y(1), along_y(2)
    values = [b + h for b, h in zip(both, high)] + [b + l for b, l in zip(both, low)]
    for px in range(2):
        for py in range(2):
            for pz in range(2):
                for parent in range(2):
                    at = ((px * 2 + py) * 2 + pz) * 4 + parent * 2
                    row = (2 * parent + px) * 4 + pz * 2 + py
                    t_re[pl.ds(row, 8, stride=16), :] = values[at]
                    t_im[pl.ds(row, 8, stride=16), :] = values[at + 1]

    re_high, re_low = split_bf16(t_re[...])
    im_high, im_low = split_bf16(t_im[...])
    t_high = jnp.concatenate([re_high, im_high], axis=1)
    t_low = jnp.concatenate([re_low, im_low], axis=1)
    total[...] += dot_nt(t_high, table_high) + (dot_nt(t_low, table_high) + dot_nt(t_high, table_low))

    @pl.when(step == pl.num_programs(0) - 1)
    def finish():
        for k, out_ref in enumerate((o0, o1, o2, o3)):
            base = pl.multiple_of((sub ^ k) * 32, 32)
            out_ref[...] = total[pl.ds(base, 32), :] * (1.0 / 4096.0)


def translate(place, chunks, inner, outer, w_high, w_low, kappa):
    block_count, width = w_high.shape[0], w_high.shape[1]
    whole = lambda b, p: (0, 0)
    block = lambda b, p: (b, 0, 0)
    chunk_spec = pl.BlockSpec((32, width), whole)
    halo_spec = pl.BlockSpec((64, width), whole)
    table_spec = pl.BlockSpec((1, width, 2 * LANES), block)
    f32, bf16 = jnp.float32, jnp.bfloat16
    return pl.pallas_call(
        translate_body,
        grid_spec=pltpu.PrefetchScalarGridSpec(
            num_scalar_prefetch=1,
            grid=(block_count,),
            in_specs=[chunk_spec] * 4 + [halo_spec] * 2 + [table_spec] * 2
            + [pl.BlockSpec((1, 27 * 24, LANES), block)],
            out_specs=[chunk_spec] * 4,
            scratch_shapes=[
                pltpu.VMEM((256, width), f32),
                pltpu.VMEM((256, width), bf16),
                pltpu.VMEM((256, width), bf16),
                pltpu.VMEM((320, LANES), f32),
                pltpu.VMEM((320, LANES), f32),
                pltpu.VMEM((12 * 27 * 24, LANES), f32),
                pltpu.VMEM((128, LANES), f32),
                pltpu.VMEM((128, LANES), f32),
                pltpu.VMEM((128, width), f32),
            ],
        ),
        out_shape=[jax.ShapeDtypeStruct((32, width), f32)] * 4,
        compiler_params=pltpu.CompilerParams(vmem_limit_bytes=VMEM_BYTES),
        name="translate",
    )(place, *chunks, inner, outer, w_high, w_low, kappa)


def phase_table(freq, edge_count):
    points = surface_points(edge_count)
    grid_side = 2 * edge_count
    freq_x = freq // (grid_side * grid_side)
    freq_y = freq // grid_side % grid_side
    freq_z = freq % grid_side
    at = [jnp.asarray(points[dim], jnp.int32)[None, :, None] for dim in range(3)]
    turns = (
        at[0] * freq_x[:, None, :] + at[1] * freq_y[:, None, :] + at[2] * freq_z[:, None, :]
    ) % grid_side
    angles = turns.astype(jnp.float32) * (2.0 * math.pi / grid_side)
    cosine, sine = jnp.cos(angles), jnp.sin(angles)
    top = jnp.concatenate([cosine, -sine], axis=2)
    bottom = jnp.concatenate([sine, cosine], axis=2)
    table = jnp.concatenate([top, bottom], axis=1)
    high = lax.reduce_precision(table, 8, 7)
    return high.astype(jnp.bfloat16), (table - high).astype(jnp.bfloat16)


def local(density, occupied, kernels):
    block_x, block_y, block_z, surf_count = density.shape[1:]
    slab_count = lax.axis_size("slab")
    sub_count = lax.axis_size("sub")
    freq_part = kernels.shape[-1]
    assert (block_x, block_y, block_z, sub_count) == (4, 4, 2, 4)
    slab, sub = lax.axis_index("slab"), lax.axis_index("sub")
    core = slab % 2

    def exchange(values, axis, bits):
        pairs = [(i, i ^ bits) for i in range(lax.axis_size(axis))]
        return lax.ppermute(values, axis, pairs)

    masked = jnp.where(occupied[None, :, :, :, None] > 0, density, 0.0)
    own = masked.reshape(2, 4, 2, 2, 2, surf_count).transpose(2, 1, 4, 3, 0, 5)
    own = own.reshape(32, 2 * surf_count)
    chunks = [own] + [exchange(own, "sub", k) for k in range(1, 4)]

    mine = compact_kernels(kernels)
    same_core = [mine] + [exchange(mine, "slab", m) for m in range(2, slab_count, 2)]
    packed = jnp.stack(same_core)
    other_core = exchange(packed, "slab", 1)
    gathered = jnp.concatenate([packed, other_core])
    per_block = LANES // freq_part
    block_count = slab_count // per_block
    gathered = gathered.reshape(block_count, per_block, 2, ROWS_KEPT, freq_part)
    gathered = gathered.transpose(0, 2, 3, 1, 4).reshape(block_count, 2, ROWS_KEPT, LANES)
    kappa = prepare_kernels(gathered)

    order = np.array(list(range(0, slab_count, 2)) + list(range(1, slab_count, 2)), np.int32)
    owner = slab ^ jnp.asarray(order)
    freq = (freq_part * (sub_count * owner + sub))[:, None] + jnp.arange(freq_part)[None, :]
    w_high, w_low = phase_table(freq.reshape(block_count, LANES).astype(jnp.int32), P_SIZE)

    stacked = jnp.stack(chunks).reshape(4, 2, 16, 2 * surf_count)
    inner = lax.dynamic_slice_in_dim(stacked, 8 * (1 - core), 8, 2).reshape(64, -1)
    outer = lax.dynamic_slice_in_dim(stacked, 8 * core, 8, 2).reshape(64, -1)
    inner = exchange(inner, "slab", 1)
    across = [(i, i + 1) for i in range(1, slab_count - 1, 2)]
    across += [(right, left) for left, right in across]
    outer = lax.ppermute(outer, "slab", across)

    place = jnp.stack([sub, core]).astype(jnp.int32)
    parts = translate(place, chunks, inner, outer, w_high, w_low, kappa)
    fields = parts[0]
    for k in range(1, 4):
        fields = fields + exchange(parts[k], "sub", k)
    fields = fields.reshape(2, 4, 2, 2, 2, surf_count).transpose(4, 1, 0, 3, 2, 5)
    fields = fields.reshape(2, block_x, block_y, block_z, surf_count)
    return jnp.where(occupied[None, :, :, :, None] > 0, fields, 0.0)


def solution(mesh):
    return jax.shard_map(
        local,
        mesh=mesh,
        in_specs=(
            P(None, "slab", "sub", None, None),
            P("slab", "sub", None),
            P(None, None, ("slab", "sub")),
        ),
        out_specs=P(None, "slab", "sub", None, None),
        check_vma=False,
    )
```

```python
import functools
import math

import jax
import jax.numpy as jnp
import numpy as np
from jax import lax
from jax.experimental import pallas as pl
from jax.experimental.pallas import tpu as pltpu
from jax.sharding import PartitionSpec as P

P_SIZE = 8
LANES = 128
COLUMNS = 5
VMEM_BYTES = 56 * 1024 * 1024
NEIGHBOURS = [(ex, ey) for ex in (-1, 0, 1) for ey in (-1, 0, 1) if (ex, ey) != (0, 0)]


def surface_points(edge_count):
    rows_found = []
    for first in range(edge_count):
        for second in range(edge_count):
            for third in range(edge_count):
                if min(first, second, third) == 0 or max(first, second, third) == edge_count - 1:
                    rows_found.append((first, second, third))
    return np.array(rows_found, dtype=np.int32).T


def offset_slots():
    slots = {}
    for step_x in range(-3, 4):
        for step_y in range(-3, 4):
            for step_z in range(-3, 4):
                if max(abs(step_x), abs(step_y), abs(step_z)) > 1:
                    slots[step_x, step_y, step_z] = len(slots)
    return slots


def column_groups():
    slots = offset_slots()
    return {key[:2]: slot for key, slot in slots.items() if key[2] == -1}


GROUPS = column_groups()
GROUP_ROW = {key: 3 * place for place, key in enumerate(GROUPS)}
KEPT = 3 * len(GROUPS)
KEPT_PADDED = 128


def expansion():
    weights = ((1, -1, 0), (0, -1, 1), (0, 1, 0))
    found = np.zeros((27 * 8, KEPT_PADDED), np.float32)
    for comp in range(27):
        cx, cy, cz = comp // 9, comp // 3 % 3, comp % 3
        for place, (ex, ey) in enumerate(NEIGHBOURS):
            for ax in range(3):
                for ay in range(3):
                    row = GROUP_ROW.get((2 * ex + ax - 1, 2 * ey + ay - 1))
                    if row is not None:
                        for az in range(3):
                            found[comp * 8 + place, row + az] += weights[cx][ax] * weights[cy][ay] * weights[cz][az]
    return found


def compact_body(kernel_ref, out_ref, held, sem):
    copy = pltpu.make_async_copy(kernel_ref, held, sem)
    copy.start()
    copy.wait()
    for key, slot in GROUPS.items():
        row = 2 * GROUP_ROW[key]
        out_ref[row:row + 6, :] = held[2 * slot:2 * slot + 6, :]


def compact_kernels(kernels):
    rows, width = kernels.shape[1:]
    return pl.pallas_call(
        compact_body,
        in_specs=[pl.BlockSpec(memory_space=pl.ANY)],
        out_specs=pl.BlockSpec(memory_space=pltpu.VMEM),
        out_shape=jax.ShapeDtypeStruct((2 * KEPT, width), jnp.float32),
        scratch_shapes=[pltpu.VMEM((2 * rows, width), jnp.float32), pltpu.SemaphoreType.DMA],
        name="compact",
    )(kernels.transpose(1, 0, 2).reshape(2 * rows, width))


def row_of(x, y, z):
    return (y // 2) * 16 + x * 4 + z * 2 + y % 2


def layer_start(x):
    return 64 + 28 * (x - 1)


def pack_body(occupied_ref, density_ref, out_ref, rows_re, rows_im):
    for x in range(4):
        for y in range(4):
            for z in range(2):
                keep = occupied_ref[x, z:z + 1, y:y + 1] > 0
                row = row_of(x, y, z)
                for part, rows in enumerate((rows_re, rows_im)):
                    values = density_ref[part, x, y, z:z + 1, :]
                    rows[row:row + 1, :] = jnp.where(keep, values, 0.0)
    parts = (rows_re[...], rows_im[...])
    gap = jnp.zeros((32, 4), jnp.float32)
    columns = [
        [part[:, 0:64] for part in parts],
        [part[:, 232:296] for part in parts],
    ]
    for x in (1, 3, 5):
        pieces = []
        for part in parts:
            for layer in (x, x + 1):
                at = layer_start(layer)
                pieces += [part[:, at:at + 28], gap]
        columns.append(pieces)
    for place, pieces in enumerate(columns):
        out_ref[:, place * LANES:(place + 1) * LANES] = jnp.concatenate(pieces, axis=1)


def pack(occupied, density):
    width = density.shape[-1]
    return pl.pallas_call(
        pack_body,
        in_specs=[pl.BlockSpec(memory_space=pltpu.VMEM), pl.BlockSpec(memory_space=pltpu.VMEM)],
        out_specs=pl.BlockSpec(memory_space=pltpu.VMEM),
        out_shape=jax.ShapeDtypeStruct((32, COLUMNS * LANES), jnp.float32),
        scratch_shapes=[pltpu.VMEM((32, width), jnp.float32)] * 2,
        name="pack",
    )(occupied.transpose(0, 2, 1), density)


def unpack_body(occupied_ref, p0, p1, p2, p3, out_ref, rows_re, rows_im):
    values = (p0[...] + p1[...]) + (p2[...] + p3[...])
    for part, rows in enumerate((rows_re, rows_im)):
        base = 64 * part
        pieces = [values[:, base:base + 64]]
        for layer in range(6):
            at = (2 + layer // 2) * LANES + base + 32 * (layer % 2)
            pieces.append(values[:, at:at + 28])
        pieces.append(values[:, LANES + base:LANES + base + 64])
        rows[...] = jnp.concatenate(pieces, axis=1)
    for x in range(4):
        for y in range(4):
            for z in range(2):
                keep = occupied_ref[x, z:z + 1, y:y + 1] > 0
                row = row_of(x, y, z)
                for part, rows in enumerate((rows_re, rows_im)):
                    out_ref[part, x, y, z:z + 1, :] = jnp.where(keep, rows[row:row + 1, :], 0.0)


def unpack(occupied, parts, shape):
    in_vmem = pl.BlockSpec(memory_space=pltpu.VMEM)
    return pl.pallas_call(
        unpack_body,
        in_specs=[pl.BlockSpec(memory_space=pltpu.VMEM)] + [in_vmem] * 4,
        out_specs=in_vmem,
        out_shape=jax.ShapeDtypeStruct(shape, jnp.float32),
        scratch_shapes=[pltpu.VMEM((32, shape[-1]), jnp.float32)] * 2,
        name="unpack",
    )(occupied.transpose(0, 2, 1), *parts)


def split_bf16(values):
    high = values.astype(jnp.bfloat16)
    low = (values - high.astype(jnp.float32)).astype(jnp.bfloat16)
    return high, low


def translate_body(
    sub_count, freq_part,
    c0, c1, c2, c3, inner_ref, outer_ref, factor_ref, matrix_ref, table_ref, *refs,
):
    block_count = len(refs) - 4 - 14
    block_refs, (o0, o1, o2, o3) = refs[:block_count], refs[block_count:block_count + 4]
    (
        rows, rolled, layers, spectra, comps, sums, split_sums, moved, total, tables, raw, pieces_in, kernel_ref, sems,
    ) = refs[block_count + 4:]
    slab, sub = lax.axis_index("slab"), lax.axis_index("sub")
    core = lax.rem(slab, 2)
    half_blocks = block_count // 2
    piece_count = LANES // freq_part
    class_count = tables.shape[0] // piece_count
    class_blocks = block_count // class_count
    plane = 4 * P_SIZE * P_SIZE

    variant = lax.div(lax.rem(freq_part * sub, plane), LANES) if table_ref.shape[0] > 1 else 0
    copies = [pltpu.make_async_copy(table_ref.at[variant], tables, sems.at[block_count])]
    for block, ref in enumerate(block_refs):
        copies.append(pltpu.make_async_copy(ref, raw.at[block], sems.at[block]))
    for copy in copies:
        copy.start()

    for k, chunk in enumerate((c0, c1, c2, c3)):
        source = sub ^ k
        for half in range(2):
            base = pl.multiple_of((2 * source + half) * 32, 32)
            rows[pl.ds(base + 8, 16), :] = chunk[half * 16:half * 16 + 16, :]
            at = k * 16 + half * 8
            rows[pl.ds(pl.multiple_of(base + 24 * (1 - core), 8), 8), :] = inner_ref[at:at + 8, :]
            rows[pl.ds(pl.multiple_of(base + 24 * core, 8), 8), :] = outer_ref[at:at + 8, :]
    for place in range(1, COLUMNS):
        lanes = slice(place * LANES, (place + 1) * LANES)
        for at in range(0, 256, 32):
            rolled[at:at + 32, lanes] = pltpu.roll(rows[at:at + 32, lanes], 64, 1)
    edge = jnp.zeros((54, LANES), jnp.float32)
    for parent in range(4):
        for place in (0, 9):
            at = (parent * 10 + place) * 54
            comps[at:at + 54, :] = edge
    total[...] = jnp.zeros_like(total)

    def split_store(ref, at, place, values):
        high, low = split_bf16(values)
        for third, piece in enumerate((high, low, high)):
            lanes = third * 256 + place * LANES
            ref[pl.ds(at, 16), lanes:lanes + LANES] = piece

    def factors(block, piece):
        odd = (block >= half_blocks).astype(jnp.int32)
        owner = slab ^ (2 * ((block - half_blocks * odd) * piece_count + piece) + odd)
        freq_x = lax.div(freq_part * (sub_count * owner + sub), plane)
        return [factor_ref[freq_x, row:row + 1, :] for row in range(8)]

    pieces_in[...] = jnp.zeros_like(pieces_in)

    for group in range(class_count):
        for piece in range(piece_count):

            def transform_x(index, _):
                factor = factors(group * class_blocks + index, piece)
                for at in range(0, 256, 16):
                    def column(ref, place):
                        return ref[at:at + 16, place * LANES:(place + 1) * LANES]

                    full = column(rows, 0) + (factor[0] * column(rows, 1) + factor[1] * column(rolled, 1))
                    ring = None
                    for pair in range(3):
                        term = (
                            factor[2 + 2 * pair] * column(rows, 2 + pair)
                            + factor[3 + 2 * pair] * column(rolled, 2 + pair)
                        )
                        ring = term if ring is None else ring + term
                    target = pl.multiple_of(index * 256 + at, 16)
                    split_store(layers, target, 0, full)
                    split_store(layers, target, 1, ring)
                return 0

            lax.fori_loop(0, class_blocks, transform_x, 0)
            if group == 0 and piece == 0:
                copies[0].wait()
            found = jnp.dot(layers[...], tables[group * piece_count + piece, 0], preferred_element_type=jnp.float32)
            span = slice(group * class_blocks * 256, (group + 1) * class_blocks * 256)
            for part in range(2):
                values = found[:, part * LANES:(part + 1) * LANES]
                if piece > 0:
                    values = values + spectra[part, span, :]
                spectra[part, span, :] = values

    for copy in copies[1:]:
        copy.wait()

    def expand(block, _):
        for part in range(2):
            left = raw[block, pl.ds(part, KEPT, stride=2), :]
            lanes = slice(part * LANES, (part + 1) * LANES)
            for turn in range(3):
                piece = left.astype(jnp.bfloat16)
                left = left - piece.astype(jnp.float32)
                pieces_in[turn * KEPT_PADDED:turn * KEPT_PADDED + KEPT, lanes] = piece
        result = jnp.dot(matrix_ref[...], pieces_in[...], preferred_element_type=jnp.float32)
        for part in range(2):
            kernel_ref[block, part] = result[:, part * LANES:(part + 1) * LANES]
        return 0

    lax.fori_loop(0, block_count, expand, 0)

    def translate_block(block):
        for parent in range(4):
            values = np.empty((2, 3, 3, 3), dtype=object)
            for part in range(2):
                for px in range(2):
                    for py in range(2):
                        for pz in range(2):
                            row = block * 256 + (2 * parent + px) * 4 + pz * 2 + py
                            values[part, px, py, pz] = spectra[part, pl.ds(row, 8, stride=32), :]
                for px in range(2):
                    for py in range(2):
                        values[part, px, py, 2] = values[part, px, py, 0] + values[part, px, py, 1]
                    for cz in range(3):
                        values[part, px, 2, cz] = values[part, px, 0, cz] + values[part, px, 1, cz]
                for cy in range(3):
                    for cz in range(3):
                        values[part, 2, cy, cz] = values[part, 0, cy, cz] + values[part, 1, cy, cz]
            for comp in range(27):
                for part in range(2):
                    value = values[part, comp // 9, comp // 3 % 3, comp % 3]
                    comps[pl.ds((parent * 10 + 1) * 54 + comp * 2 + part, 8, stride=54), :] = value

        def product(cx, cy, cz):
            comp = (cx * 3 + cy) * 3 + cz
            have = [[None, None] for _ in range(2)]
            for ey in (-1, 0, 1):
                source = []
                for parent in range(4):
                    at = (parent * 10 + 1 + ey) * 54 + comp * 2
                    source.append([comps[pl.ds(at + part, 8, stride=54), :] for part in range(2)])
                for place, (ex, neighbour_y) in enumerate(NEIGHBOURS):
                    if neighbour_y != ey:
                        continue
                    row = comp * 8 + place
                    k_re, k_im = (
                        jnp.broadcast_to(kernel_ref[block, part, row:row + 1, :], (8, LANES)) for part in range(2)
                    )
                    for parent in range(2):
                        s_re, s_im = source[parent + 1 + ex]
                        terms = (k_re * s_re - k_im * s_im, k_re * s_im + k_im * s_re)
                        for part in range(2):
                            old = have[parent][part]
                            have[parent][part] = terms[part] if old is None else old + terms[part]
            return have[0] + have[1]

        def merge(low, high, both):
            return [b + h for b, h in zip(both, high)] + [b + l for b, l in zip(both, low)]

        def along_z(cx, cy):
            return merge(product(cx, cy, 0), product(cx, cy, 1), product(cx, cy, 2))

        def along_y(cx):
            return merge(along_z(cx, 0), along_z(cx, 1), along_z(cx, 2))

        values = merge(along_y(0), along_y(1), along_y(2))
        for px in range(2):
            for py in range(2):
                for pz in range(2):
                    for parent in range(2):
                        at = ((px * 2 + py) * 2 + pz) * 4 + parent * 2
                        row = (2 * parent + px) * 4 + pz * 2 + py
                        for part in range(2):
                            sums[part, pl.ds(row, 8, stride=16), :] = values[at + part]
        for at in range(0, 128, 16):
            for part in range(2):
                split_store(split_sums, pl.multiple_of(block * 128 + at, 16), part, sums[part, at:at + 16, :])

    def one_block(block, _):
        translate_block(block)
        return 0

    lax.fori_loop(0, block_count, one_block, 0)

    for group in range(class_count):
        span = slice(group * class_blocks * 128, (group + 1) * class_blocks * 128)
        for piece in range(piece_count):
            moved[...] = jnp.dot(split_sums[span, :], tables[group * piece_count + piece, 1], preferred_element_type=jnp.float32)

            def transform_back(index, _):
                factor = factors(group * class_blocks + index, piece)
                for at in range(0, 128, 16):
                    source = pl.ds(pl.multiple_of(index * 128 + at, 16), 16)
                    full, ring = moved[source, :LANES], moved[source, LANES:]
                    full_rolled, ring_rolled = pltpu.roll(full, 64, 1), pltpu.roll(ring, 64, 1)
                    total[at:at + 16, 0:LANES] += full
                    total[at:at + 16, LANES:2 * LANES] += factor[0] * full - factor[1] * full_rolled
                    for pair in range(3):
                        lanes = slice((2 + pair) * LANES, (3 + pair) * LANES)
                        total[at:at + 16, lanes] += (
                            factor[2 + 2 * pair] * ring - factor[3 + 2 * pair] * ring_rolled
                        )
                return 0

            lax.fori_loop(0, class_blocks, transform_back, 0)

    for k, out_ref in enumerate((o0, o1, o2, o3)):
        base = pl.multiple_of((sub ^ k) * 32, 32)
        out_ref[...] = total[pl.ds(base, 32), :] * (1.0 / 4096.0)


def translate(sub_count, freq_part, chunks, inner, outer, tables, blocks):
    block_count = len(blocks)
    class_blocks = block_count * (LANES // freq_part) // tables.shape[1]
    width = COLUMNS * LANES
    matrix = jnp.asarray(np.concatenate([expansion()] * 3, axis=1), jnp.bfloat16)
    f32, bf16 = jnp.float32, jnp.bfloat16
    in_vmem = pl.BlockSpec(memory_space=pltpu.VMEM)
    anywhere = pl.BlockSpec(memory_space=pl.ANY)
    return pl.pallas_call(
        functools.partial(translate_body, sub_count, freq_part),
        in_specs=[in_vmem] * 8 + [anywhere] * (1 + block_count),
        out_specs=[in_vmem] * 4,
        scratch_shapes=[
            pltpu.VMEM((256, width), f32),
            pltpu.VMEM((256, width), f32),
            pltpu.VMEM((class_blocks * 256, 768), bf16),
            pltpu.VMEM((2, block_count * 256, LANES), f32),
            pltpu.VMEM((40 * 54, LANES), f32),
            pltpu.VMEM((2, 128, LANES), f32),
            pltpu.VMEM((block_count * 128, 768), bf16),
            pltpu.VMEM((class_blocks * 128, 256), f32),
            pltpu.VMEM((128, width), f32),
            pltpu.VMEM(tables.shape[1:], bf16),
            pltpu.VMEM((block_count, 2 * KEPT, LANES), f32),
            pltpu.VMEM((3 * KEPT_PADDED, 2 * LANES), bf16),
            pltpu.VMEM((block_count, 2, 27 * 8, LANES), f32),
            pltpu.SemaphoreType.DMA((block_count + 1,)),
        ],
        out_shape=[jax.ShapeDtypeStruct((32, width), f32)] * 4,
        compiler_params=pltpu.CompilerParams(vmem_limit_bytes=VMEM_BYTES),
        name="translate",
    )(*chunks, inner, outer, jnp.asarray(layer_factors()), matrix, tables, *blocks)


def plane_layout():
    points = surface_points(P_SIZE)
    layer = points[1:, points[0] == 1]
    at_y, at_z, used, part = (np.zeros(256, np.int32) for _ in range(4))
    at_y[:128], at_z[:128] = np.arange(128) % 64 // 8, np.arange(128) % 8
    used[:128], part[:128] = 1, np.arange(128) // 64
    for half in range(2):
        for slot in range(2):
            base = 128 + 64 * half + 32 * slot
            at_y[base:base + 28], at_z[base:base + 28] = layer
            used[base:base + 28], part[base:base + 28] = 1, half
    return at_y, at_z, used, part


def plane_tables(freq, freq_part):
    side = 2 * P_SIZE
    at_y, at_z, used, part = plane_layout()
    lib = np if isinstance(freq, np.ndarray) else jnp
    freq_y, freq_z = freq // side % side, freq % side
    column = lambda values: values[None, :, None]
    turns = column(at_y) * freq_y[:, None, :] + column(at_z) * freq_z[:, None, :]
    quarter = side // 4
    turns = lib.concatenate([turns - quarter * column(part), turns + quarter * column(1 - part)], axis=2)
    values = lib.cos((turns % side).astype(np.float32) * np.float32(2.0 * math.pi / side)) * column(used.astype(np.float32))
    pieces = LANES // freq_part
    owner = np.arange(2 * LANES) % LANES // freq_part
    mine = (owner[None, :] == np.arange(pieces)[:, None]).astype(np.float32)
    values = (values[:, None] * mine[None, :, None, :]).reshape(-1, 256, 256)
    if lib is np:
        high = values.astype(jnp.bfloat16).astype(np.float32)
    else:
        high = lax.reduce_precision(values, 8, 7)
    low = values - high
    both = []
    for turned in (False, True):
        third = [lib.swapaxes(piece, 1, 2) if turned else piece for piece in (high, high, low)]
        both.append(lib.concatenate(third, axis=1))
    return lib.stack(both, axis=1).astype(jnp.bfloat16)


def layer_factors():
    side = 2 * P_SIZE
    lane = np.arange(LANES)
    layer = np.stack([np.full(LANES, 7)] + [2 * pair + 1 + lane % 64 // 32 for pair in range(3)])
    sign = np.where(lane < 64, 1.0, -1.0)
    angles = (layer[None] * np.arange(side)[:, None, None] % side) * (2.0 * math.pi / side)
    both = np.stack([np.cos(angles), np.sin(angles) * sign], axis=2)
    return both.reshape(side, 8, LANES).astype(np.float32)


def local(density, occupied, kernels):
    block_x, block_y, block_z, surf_count = density.shape[1:]
    slab_count = lax.axis_size("slab")
    sub_count = lax.axis_size("sub")
    freq_part = kernels.shape[-1]
    assert (block_x, block_y, block_z, sub_count) == (4, 4, 2, 4)
    slab, sub = lax.axis_index("slab"), lax.axis_index("sub")
    core = slab % 2

    def exchange(values, axis, bits):
        pairs = [(i, i ^ bits) for i in range(lax.axis_size(axis))]
        return lax.ppermute(values, axis, pairs)

    own = pack(occupied, density)
    width = own.shape[-1]
    chunks = [own] + [exchange(own, "sub", k) for k in range(1, 4)]

    mine = compact_kernels(kernels)
    same_core = [mine] + [exchange(mine, "slab", m) for m in range(2, slab_count, 2)]

    same_core, chunks = lax.optimization_barrier((same_core, chunks))

    def rows_at(start):
        parts = [lax.dynamic_slice_in_dim(chunk.reshape(2, 16, width), start, 8, 1) for chunk in chunks]
        return jnp.concatenate(parts).reshape(64, width)

    across = [(i, i + 1) for i in range(1, slab_count - 1, 2)]
    across += [(right, left) for left, right in across]
    outer = lax.ppermute(rows_at(8 * core), "slab", across)
    inner = exchange(rows_at(8 * (1 - core)), "slab", 1)

    other_core = [exchange(block, "slab", 1) for block in same_core]
    pieces = LANES // freq_part
    block_count = slab_count // pieces

    def by_block(blocks):
        return [jnp.concatenate(blocks[at:at + pieces], axis=1) for at in range(0, len(blocks), pieces)]

    blocks = same_core + other_core if pieces == 1 else by_block(same_core) + by_block(other_core)
    plane = 4 * P_SIZE * P_SIZE
    if pieces == 1 and (freq_part * sub_count) % plane == 0:
        freq = np.arange(plane, dtype=np.int32).reshape(-1, LANES)
        tables = jnp.asarray(plane_tables(freq, freq_part))[:, None]
    else:
        owner = slab ^ jnp.asarray([2 * k + half for half in range(2) for k in range(pieces)], jnp.int32)
        base = freq_part * (sub_count * owner + sub)
        freq = (base[:, None] + jnp.arange(freq_part)[None, :]).reshape(2, LANES).astype(jnp.int32)
        tables = plane_tables(freq, freq_part)[None]

    parts = translate(sub_count, freq_part, chunks, inner, outer, tables, blocks)
    fields = [parts[0]] + [exchange(parts[k], "sub", k) for k in range(1, 4)]
    return unpack(occupied, fields, density.shape)


def solution(mesh):
    return jax.shard_map(
        local,
        mesh=mesh,
        in_specs=(
            P(None, "slab", "sub", None, None),
            P("slab", "sub", None),
            P(None, None, ("slab", "sub")),
        ),
        out_specs=P(None, "slab", "sub", None, None),
        check_vma=False,
    )
```

```python
import functools
import math

import jax
import jax.numpy as jnp
import numpy as np
from jax import lax
from jax.experimental import pallas as pl
from jax.experimental.pallas import tpu as pltpu
from jax.sharding import PartitionSpec as P

P_SIZE = 8
LANES = 128
COLUMNS = 5
VMEM_BYTES = 56 * 1024 * 1024
NEIGHBOURS = [(ex, ey) for ex in (-1, 0, 1) for ey in (-1, 0, 1) if (ex, ey) != (0, 0)]


def surface_points(edge_count):
    rows_found = []
    for first in range(edge_count):
        for second in range(edge_count):
            for third in range(edge_count):
                if min(first, second, third) == 0 or max(first, second, third) == edge_count - 1:
                    rows_found.append((first, second, third))
    return np.array(rows_found, dtype=np.int32).T


def offset_slots():
    slots = {}
    for step_x in range(-3, 4):
        for step_y in range(-3, 4):
            for step_z in range(-3, 4):
                if max(abs(step_x), abs(step_y), abs(step_z)) > 1:
                    slots[step_x, step_y, step_z] = len(slots)
    return slots


def column_groups():
    slots = offset_slots()
    return {key[:2]: slot for key, slot in slots.items() if key[2] == -1}


GROUPS = column_groups()
GROUP_ROW = {key: 3 * place for place, key in enumerate(GROUPS)}
KEPT = 3 * len(GROUPS)
KEPT_PADDED = 128


def expansion():
    weights = ((1, -1, 0), (0, -1, 1), (0, 1, 0))
    found = np.zeros((27 * 8, KEPT_PADDED), np.float32)
    for comp in range(27):
        cx, cy, cz = comp // 9, comp // 3 % 3, comp % 3
        for place, (ex, ey) in enumerate(NEIGHBOURS):
            for ax in range(3):
                for ay in range(3):
                    row = GROUP_ROW.get((2 * ex + ax - 1, 2 * ey + ay - 1))
                    if row is not None:
                        for az in range(3):
                            found[comp * 8 + place, row + az] += weights[cx][ax] * weights[cy][ay] * weights[cz][az]
    return found


def compact_body(kernel_ref, out_ref, held, sem):
    copy = pltpu.make_async_copy(kernel_ref, held, sem)
    copy.start()
    copy.wait()
    for key, slot in GROUPS.items():
        row = 2 * GROUP_ROW[key]
        out_ref[row:row + 6, :] = held[2 * slot:2 * slot + 6, :]


def compact_kernels(kernels):
    rows, width = kernels.shape[1:]
    return pl.pallas_call(
        compact_body,
        in_specs=[pl.BlockSpec(memory_space=pl.ANY)],
        out_specs=pl.BlockSpec(memory_space=pltpu.VMEM),
        out_shape=jax.ShapeDtypeStruct((2 * KEPT, width), jnp.float32),
        scratch_shapes=[pltpu.VMEM((2 * rows, width), jnp.float32), pltpu.SemaphoreType.DMA],
        name="compact",
    )(kernels.transpose(1, 0, 2).reshape(2 * rows, width))


def row_of(x, y, z):
    return (y // 2) * 16 + x * 4 + z * 2 + y % 2


def layer_start(x):
    return 64 + 28 * (x - 1)


def pack_body(occupied_ref, density_ref, out_ref, rows_re, rows_im):
    for x in range(4):
        for y in range(4):
            for z in range(2):
                keep = occupied_ref[x, z:z + 1, y:y + 1] > 0
                row = row_of(x, y, z)
                for part, rows in enumerate((rows_re, rows_im)):
                    values = density_ref[part, x, y, z:z + 1, :]
                    rows[row:row + 1, :] = jnp.where(keep, values, 0.0)
    parts = (rows_re[...], rows_im[...])
    gap = jnp.zeros((32, 4), jnp.float32)
    columns = [
        [part[:, 0:64] for part in parts],
        [part[:, 232:296] for part in parts],
    ]
    for x in (1, 3, 5):
        pieces = []
        for part in parts:
            for layer in (x, x + 1):
                at = layer_start(layer)
                pieces += [part[:, at:at + 28], gap]
        columns.append(pieces)
    for place, pieces in enumerate(columns):
        out_ref[:, place * LANES:(place + 1) * LANES] = jnp.concatenate(pieces, axis=1)


def pack(occupied, density):
    width = density.shape[-1]
    return pl.pallas_call(
        pack_body,
        in_specs=[pl.BlockSpec(memory_space=pltpu.VMEM), pl.BlockSpec(memory_space=pltpu.VMEM)],
        out_specs=pl.BlockSpec(memory_space=pltpu.VMEM),
        out_shape=jax.ShapeDtypeStruct((32, COLUMNS * LANES), jnp.float32),
        scratch_shapes=[pltpu.VMEM((32, width), jnp.float32)] * 2,
        name="pack",
    )(occupied.transpose(0, 2, 1), density)


def unpack_body(occupied_ref, p0, p1, p2, p3, out_ref, rows_re, rows_im):
    values = (p0[...] + p1[...]) + (p2[...] + p3[...])
    for part, rows in enumerate((rows_re, rows_im)):
        base = 64 * part
        pieces = [values[:, base:base + 64]]
        for layer in range(6):
            at = (2 + layer // 2) * LANES + base + 32 * (layer % 2)
            pieces.append(values[:, at:at + 28])
        pieces.append(values[:, LANES + base:LANES + base + 64])
        rows[...] = jnp.concatenate(pieces, axis=1)
    for x in range(4):
        for y in range(4):
            for z in range(2):
                keep = occupied_ref[x, z:z + 1, y:y + 1] > 0
                row = row_of(x, y, z)
                for part, rows in enumerate((rows_re, rows_im)):
                    out_ref[part, x, y, z:z + 1, :] = jnp.where(keep, rows[row:row + 1, :], 0.0)


def unpack(occupied, parts, shape):
    in_vmem = pl.BlockSpec(memory_space=pltpu.VMEM)
    return pl.pallas_call(
        unpack_body,
        in_specs=[pl.BlockSpec(memory_space=pltpu.VMEM)] + [in_vmem] * 4,
        out_specs=in_vmem,
        out_shape=jax.ShapeDtypeStruct(shape, jnp.float32),
        scratch_shapes=[pltpu.VMEM((32, shape[-1]), jnp.float32)] * 2,
        name="unpack",
    )(occupied.transpose(0, 2, 1), *parts)


def split_bf16(values):
    high = values.astype(jnp.bfloat16)
    low = (values - high.astype(jnp.float32)).astype(jnp.bfloat16)
    return high, low


def translate_body(
    sub_count, freq_part,
    c0, c1, c2, c3, inner_ref, outer_ref, factor_ref, matrix_ref, table_ref, *refs,
):
    block_count = len(refs) - 4 - 13
    block_refs, (o0, o1, o2, o3) = refs[:block_count], refs[block_count:block_count + 4]
    (
        rows, rolled, layers, spectra, comps, sums, split_sums, moved, total, tables, pieces_in, kernel_ref, sem,
    ) = refs[block_count + 4:]
    slab, sub = lax.axis_index("slab"), lax.axis_index("sub")
    core = lax.rem(slab, 2)
    half_blocks = block_count // 2
    piece_count = LANES // freq_part
    class_count = tables.shape[0] // piece_count
    class_blocks = block_count // class_count
    plane = 4 * P_SIZE * P_SIZE

    variant = lax.div(lax.rem(freq_part * sub, plane), LANES) if table_ref.shape[0] > 1 else 0
    copy = pltpu.make_async_copy(table_ref.at[variant], tables, sem)
    copy.start()

    for k, chunk in enumerate((c0, c1, c2, c3)):
        source = sub ^ k
        for half in range(2):
            base = pl.multiple_of((2 * source + half) * 32, 32)
            rows[pl.ds(base + 8, 16), :] = chunk[half * 16:half * 16 + 16, :]
            at = k * 16 + half * 8
            rows[pl.ds(pl.multiple_of(base + 24 * (1 - core), 8), 8), :] = inner_ref[at:at + 8, :]
            rows[pl.ds(pl.multiple_of(base + 24 * core, 8), 8), :] = outer_ref[at:at + 8, :]
    for place in range(1, COLUMNS):
        lanes = slice(place * LANES, (place + 1) * LANES)
        for at in range(0, 256, 32):
            rolled[at:at + 32, lanes] = pltpu.roll(rows[at:at + 32, lanes], 64, 1)
    edge = jnp.zeros((54, LANES), jnp.float32)
    for parent in range(4):
        for place in (0, 9):
            at = (parent * 10 + place) * 54
            comps[at:at + 54, :] = edge
    total[...] = jnp.zeros_like(total)

    def split_store(ref, at, place, values):
        high, low = split_bf16(values)
        for third, piece in enumerate((high, low, high)):
            lanes = third * 256 + place * LANES
            ref[pl.ds(at, 16), lanes:lanes + LANES] = piece

    def factors(block, piece):
        odd = (block >= half_blocks).astype(jnp.int32)
        owner = slab ^ (2 * ((block - half_blocks * odd) * piece_count + piece) + odd)
        freq_x = lax.div(freq_part * (sub_count * owner + sub), plane)
        return [factor_ref[freq_x, row:row + 1, :] for row in range(8)]

    pieces_in[...] = jnp.zeros_like(pieces_in)

    for group in range(class_count):
        for piece in range(piece_count):

            def transform_x(index, _):
                factor = factors(group * class_blocks + index, piece)
                for at in range(0, 256, 16):
                    def column(ref, place):
                        return ref[at:at + 16, place * LANES:(place + 1) * LANES]

                    full = column(rows, 0) + (factor[0] * column(rows, 1) + factor[1] * column(rolled, 1))
                    ring = None
                    for pair in range(3):
                        term = (
                            factor[2 + 2 * pair] * column(rows, 2 + pair)
                            + factor[3 + 2 * pair] * column(rolled, 2 + pair)
                        )
                        ring = term if ring is None else ring + term
                    target = pl.multiple_of(index * 256 + at, 16)
                    split_store(layers, target, 0, full)
                    split_store(layers, target, 1, ring)
                return 0

            lax.fori_loop(0, class_blocks, transform_x, 0)
            if group == 0 and piece == 0:
                copy.wait()
            found = jnp.dot(layers[...], tables[group * piece_count + piece, 0], preferred_element_type=jnp.float32)
            span = slice(group * class_blocks * 256, (group + 1) * class_blocks * 256)
            for part in range(2):
                values = found[:, part * LANES:(part + 1) * LANES]
                if piece > 0:
                    values = values + spectra[part, span, :]
                spectra[part, span, :] = values

    for block in range(block_count):
        for part in range(2):
            left = block_refs[block][pl.ds(part, KEPT, stride=2), :]
            lanes = slice(part * LANES, (part + 1) * LANES)
            for turn in range(3):
                piece = left.astype(jnp.bfloat16)
                left = left - piece.astype(jnp.float32)
                pieces_in[block % 2, turn * KEPT_PADDED:turn * KEPT_PADDED + KEPT, lanes] = piece
        result = jnp.dot(matrix_ref[...], pieces_in[block % 2], preferred_element_type=jnp.float32)
        for part in range(2):
            kernel_ref[block, part] = result[:, part * LANES:(part + 1) * LANES]

    def translate_block(block):
        for parent in range(4):
            values = np.empty((2, 3, 3, 3), dtype=object)
            for part in range(2):
                for px in range(2):
                    for py in range(2):
                        for pz in range(2):
                            row = block * 256 + (2 * parent + px) * 4 + pz * 2 + py
                            values[part, px, py, pz] = spectra[part, pl.ds(row, 8, stride=32), :]
                for px in range(2):
                    for py in range(2):
                        values[part, px, py, 2] = values[part, px, py, 0] + values[part, px, py, 1]
                    for cz in range(3):
                        values[part, px, 2, cz] = values[part, px, 0, cz] + values[part, px, 1, cz]
                for cy in range(3):
                    for cz in range(3):
                        values[part, 2, cy, cz] = values[part, 0, cy, cz] + values[part, 1, cy, cz]
            for comp in range(27):
                for part in range(2):
                    value = values[part, comp // 9, comp // 3 % 3, comp % 3]
                    comps[pl.ds((parent * 10 + 1) * 54 + comp * 2 + part, 8, stride=54), :] = value

        def product(cx, cy, cz):
            comp = (cx * 3 + cy) * 3 + cz
            have = [[None, None] for _ in range(2)]
            for ey in (-1, 0, 1):
                source = []
                for parent in range(4):
                    at = (parent * 10 + 1 + ey) * 54 + comp * 2
                    source.append([comps[pl.ds(at + part, 8, stride=54), :] for part in range(2)])
                for place, (ex, neighbour_y) in enumerate(NEIGHBOURS):
                    if neighbour_y != ey:
                        continue
                    row = comp * 8 + place
                    k_re, k_im = (
                        jnp.broadcast_to(kernel_ref[block, part, row:row + 1, :], (8, LANES)) for part in range(2)
                    )
                    for parent in range(2):
                        s_re, s_im = source[parent + 1 + ex]
                        terms = (k_re * s_re - k_im * s_im, k_re * s_im + k_im * s_re)
                        for part in range(2):
                            old = have[parent][part]
                            have[parent][part] = terms[part] if old is None else old + terms[part]
            return have[0] + have[1]

        def merge(low, high, both):
            return [b + h for b, h in zip(both, high)] + [b + l for b, l in zip(both, low)]

        def along_z(cx, cy):
            return merge(product(cx, cy, 0), product(cx, cy, 1), product(cx, cy, 2))

        def along_y(cx):
            return merge(along_z(cx, 0), along_z(cx, 1), along_z(cx, 2))

        values = merge(along_y(0), along_y(1), along_y(2))
        for px in range(2):
            for py in range(2):
                for pz in range(2):
                    for parent in range(2):
                        at = ((px * 2 + py) * 2 + pz) * 4 + parent * 2
                        row = (2 * parent + px) * 4 + pz * 2 + py
                        for part in range(2):
                            sums[part, pl.ds(row, 8, stride=16), :] = values[at + part]
        for at in range(0, 128, 16):
            for part in range(2):
                split_store(split_sums, pl.multiple_of(block * 128 + at, 16), part, sums[part, at:at + 16, :])

    def one_block(block, _):
        translate_block(block)
        return 0

    lax.fori_loop(0, block_count, one_block, 0)

    for group in range(class_count):
        span = slice(group * class_blocks * 128, (group + 1) * class_blocks * 128)
        for piece in range(piece_count):
            moved[...] = jnp.dot(split_sums[span, :], tables[group * piece_count + piece, 1], preferred_element_type=jnp.float32)

            def transform_back(index, _):
                factor = factors(group * class_blocks + index, piece)
                for at in range(0, 128, 16):
                    source = pl.ds(pl.multiple_of(index * 128 + at, 16), 16)
                    full, ring = moved[source, :LANES], moved[source, LANES:]
                    full_rolled, ring_rolled = pltpu.roll(full, 64, 1), pltpu.roll(ring, 64, 1)
                    total[at:at + 16, 0:LANES] += full
                    total[at:at + 16, LANES:2 * LANES] += factor[0] * full - factor[1] * full_rolled
                    for pair in range(3):
                        lanes = slice((2 + pair) * LANES, (3 + pair) * LANES)
                        total[at:at + 16, lanes] += (
                            factor[2 + 2 * pair] * ring - factor[3 + 2 * pair] * ring_rolled
                        )
                return 0

            lax.fori_loop(0, class_blocks, transform_back, 0)

    for k, out_ref in enumerate((o0, o1, o2, o3)):
        base = pl.multiple_of((sub ^ k) * 32, 32)
        out_ref[...] = total[pl.ds(base, 32), :] * (1.0 / 4096.0)


def translate(sub_count, freq_part, chunks, inner, outer, tables, blocks):
    block_count = len(blocks)
    class_blocks = block_count * (LANES // freq_part) // tables.shape[1]
    width = COLUMNS * LANES
    matrix = jnp.asarray(np.concatenate([expansion()] * 3, axis=1), jnp.bfloat16)
    f32, bf16 = jnp.float32, jnp.bfloat16
    in_vmem = pl.BlockSpec(memory_space=pltpu.VMEM)
    anywhere = pl.BlockSpec(memory_space=pl.ANY)
    return pl.pallas_call(
        functools.partial(translate_body, sub_count, freq_part),
        in_specs=[in_vmem] * 8 + [anywhere] + [in_vmem] * block_count,
        out_specs=[in_vmem] * 4,
        scratch_shapes=[
            pltpu.VMEM((256, width), f32),
            pltpu.VMEM((256, width), f32),
            pltpu.VMEM((class_blocks * 256, 768), bf16),
            pltpu.VMEM((2, block_count * 256, LANES), f32),
            pltpu.VMEM((40 * 54, LANES), f32),
            pltpu.VMEM((2, 128, LANES), f32),
            pltpu.VMEM((block_count * 128, 768), bf16),
            pltpu.VMEM((class_blocks * 128, 256), f32),
            pltpu.VMEM((128, width), f32),
            pltpu.VMEM(tables.shape[1:], bf16),
            pltpu.VMEM((2, 3 * KEPT_PADDED, 2 * LANES), bf16),
            pltpu.VMEM((block_count, 2, 27 * 8, LANES), f32),
            pltpu.SemaphoreType.DMA,
        ],
        out_shape=[jax.ShapeDtypeStruct((32, width), f32)] * 4,
        compiler_params=pltpu.CompilerParams(vmem_limit_bytes=VMEM_BYTES),
        name="translate",
    )(*chunks, inner, outer, jnp.asarray(layer_factors()), matrix, tables, *blocks)


def plane_layout():
    points = surface_points(P_SIZE)
    layer = points[1:, points[0] == 1]
    at_y, at_z, used, part = (np.zeros(256, np.int32) for _ in range(4))
    at_y[:128], at_z[:128] = np.arange(128) % 64 // 8, np.arange(128) % 8
    used[:128], part[:128] = 1, np.arange(128) // 64
    for half in range(2):
        for slot in range(2):
            base = 128 + 64 * half + 32 * slot
            at_y[base:base + 28], at_z[base:base + 28] = layer
            used[base:base + 28], part[base:base + 28] = 1, half
    return at_y, at_z, used, part


def plane_tables(freq, freq_part):
    side = 2 * P_SIZE
    at_y, at_z, used, part = plane_layout()
    lib = np if isinstance(freq, np.ndarray) else jnp
    freq_y, freq_z = freq // side % side, freq % side
    column = lambda values: values[None, :, None]
    turns = column(at_y) * freq_y[:, None, :] + column(at_z) * freq_z[:, None, :]
    quarter = side // 4
    turns = lib.concatenate([turns - quarter * column(part), turns + quarter * column(1 - part)], axis=2)
    values = lib.cos((turns % side).astype(np.float32) * np.float32(2.0 * math.pi / side)) * column(used.astype(np.float32))
    pieces = LANES // freq_part
    owner = np.arange(2 * LANES) % LANES // freq_part
    mine = (owner[None, :] == np.arange(pieces)[:, None]).astype(np.float32)
    values = (values[:, None] * mine[None, :, None, :]).reshape(-1, 256, 256)
    if lib is np:
        high = values.astype(jnp.bfloat16).astype(np.float32)
    else:
        high = lax.reduce_precision(values, 8, 7)
    low = values - high
    both = []
    for turned in (False, True):
        third = [lib.swapaxes(piece, 1, 2) if turned else piece for piece in (high, high, low)]
        both.append(lib.concatenate(third, axis=1))
    return lib.stack(both, axis=1).astype(jnp.bfloat16)


def layer_factors():
    side = 2 * P_SIZE
    lane = np.arange(LANES)
    layer = np.stack([np.full(LANES, 7)] + [2 * pair + 1 + lane % 64 // 32 for pair in range(3)])
    sign = np.where(lane < 64, 1.0, -1.0)
    angles = (layer[None] * np.arange(side)[:, None, None] % side) * (2.0 * math.pi / side)
    both = np.stack([np.cos(angles), np.sin(angles) * sign], axis=2)
    return both.reshape(side, 8, LANES).astype(np.float32)


def local(density, occupied, kernels):
    block_x, block_y, block_z, surf_count = density.shape[1:]
    slab_count = lax.axis_size("slab")
    sub_count = lax.axis_size("sub")
    freq_part = kernels.shape[-1]
    assert (block_x, block_y, block_z, sub_count) == (4, 4, 2, 4)
    slab, sub = lax.axis_index("slab"), lax.axis_index("sub")
    core = slab % 2

    def exchange(values, axis, bits):
        pairs = [(i, i ^ bits) for i in range(lax.axis_size(axis))]
        return lax.ppermute(values, axis, pairs)

    own, mine = pack(occupied, density), compact_kernels(kernels)
    width = own.shape[-1]
    chunks = [own] + [exchange(own, "sub", k) for k in range(1, 4)]

    same_core = [mine] + [exchange(mine, "slab", m) for m in range(2, slab_count, 2)]

    def rows_at(start):
        parts = [lax.dynamic_slice_in_dim(chunk.reshape(2, 16, width), start, 8, 1) for chunk in chunks]
        return jnp.concatenate(parts).reshape(64, width)

    across = [(i, i + 1) for i in range(1, slab_count - 1, 2)]
    across += [(right, left) for left, right in across]
    outer, inner = rows_at(8 * core), rows_at(8 * (1 - core))
    outer, inner, same_core = lax.optimization_barrier((outer, inner, same_core))
    outer = lax.ppermute(outer, "slab", across)
    inner = exchange(inner, "slab", 1)

    other_core = [exchange(block, "slab", 1) for block in same_core]
    pieces = LANES // freq_part
    block_count = slab_count // pieces

    def by_block(blocks):
        return [jnp.concatenate(blocks[at:at + pieces], axis=1) for at in range(0, len(blocks), pieces)]

    blocks = same_core + other_core if pieces == 1 else by_block(same_core) + by_block(other_core)
    plane = 4 * P_SIZE * P_SIZE
    if pieces == 1 and (freq_part * sub_count) % plane == 0:
        freq = np.arange(plane, dtype=np.int32).reshape(-1, LANES)
        tables = jnp.asarray(plane_tables(freq, freq_part))[:, None]
    else:
        owner = slab ^ jnp.asarray([2 * k + half for half in range(2) for k in range(pieces)], jnp.int32)
        base = freq_part * (sub_count * owner + sub)
        freq = (base[:, None] + jnp.arange(freq_part)[None, :]).reshape(2, LANES).astype(jnp.int32)
        tables = plane_tables(freq, freq_part)[None]

    parts = translate(sub_count, freq_part, chunks, inner, outer, tables, blocks)
    fields = [parts[0]] + [exchange(parts[k], "sub", k) for k in (3, 2, 1)]
    return unpack(occupied, fields, density.shape)


def solution(mesh):
    return jax.shard_map(
        local,
        mesh=mesh,
        in_specs=(
            P(None, "slab", "sub", None, None),
            P("slab", "sub", None),
            P(None, None, ("slab", "sub")),
        ),
        out_specs=P(None, "slab", "sub", None, None),
        check_vma=False,
    )
```

```python
import functools
import math

import jax
import jax.numpy as jnp
import numpy as np
from jax import lax
from jax.experimental import pallas as pl
from jax.experimental.pallas import tpu as pltpu
from jax.sharding import PartitionSpec as P

P_SIZE = 8
LANES = 128
COLUMNS = 5
VMEM_BYTES = 56 * 1024 * 1024
NEIGHBOURS = [(ex, ey) for ex in (-1, 0, 1) for ey in (-1, 0, 1) if (ex, ey) != (0, 0)]


def surface_points(edge_count):
    rows_found = []
    for first in range(edge_count):
        for second in range(edge_count):
            for third in range(edge_count):
                if min(first, second, third) == 0 or max(first, second, third) == edge_count - 1:
                    rows_found.append((first, second, third))
    return np.array(rows_found, dtype=np.int32).T


def offset_slots():
    slots = {}
    for step_x in range(-3, 4):
        for step_y in range(-3, 4):
            for step_z in range(-3, 4):
                if max(abs(step_x), abs(step_y), abs(step_z)) > 1:
                    slots[step_x, step_y, step_z] = len(slots)
    return slots


def column_groups():
    slots = offset_slots()
    return {key[:2]: slot for key, slot in slots.items() if key[2] == -1}


GROUPS = column_groups()
GROUP_ROW = {key: 3 * place for place, key in enumerate(GROUPS)}
KEPT = 3 * len(GROUPS)
KEPT_PADDED = 128


def expansion():
    weights = ((1, -1, 0), (0, -1, 1), (0, 1, 0))
    found = np.zeros((27 * 8, KEPT_PADDED), np.float32)
    for comp in range(27):
        cx, cy, cz = comp // 9, comp // 3 % 3, comp % 3
        for place, (ex, ey) in enumerate(NEIGHBOURS):
            for ax in range(3):
                for ay in range(3):
                    row = GROUP_ROW.get((2 * ex + ax - 1, 2 * ey + ay - 1))
                    if row is not None:
                        for az in range(3):
                            found[comp * 8 + place, row + az] += weights[cx][ax] * weights[cy][ay] * weights[cz][az]
    return found


def compact_body(kernel_ref, out_ref, held, sem):
    copy = pltpu.make_async_copy(kernel_ref, held, sem)
    copy.start()
    copy.wait()
    for key, slot in GROUPS.items():
        row = 2 * GROUP_ROW[key]
        out_ref[row:row + 6, :] = held[2 * slot:2 * slot + 6, :]


def compact_kernels(kernels):
    rows, width = kernels.shape[1:]
    return pl.pallas_call(
        compact_body,
        in_specs=[pl.BlockSpec(memory_space=pl.ANY)],
        out_specs=pl.BlockSpec(memory_space=pltpu.VMEM),
        out_shape=jax.ShapeDtypeStruct((2 * KEPT, width), jnp.float32),
        scratch_shapes=[pltpu.VMEM((2 * rows, width), jnp.float32), pltpu.SemaphoreType.DMA],
        name="compact",
    )(kernels.transpose(1, 0, 2).reshape(2 * rows, width))


def row_of(x, y, z):
    return (y // 2) * 16 + x * 4 + z * 2 + y % 2


def layer_start(x):
    return 64 + 28 * (x - 1)


def pack_body(occupied_ref, density_ref, out_ref, rows_re, rows_im):
    for x in range(4):
        for y in range(4):
            for z in range(2):
                keep = occupied_ref[x, z:z + 1, y:y + 1] > 0
                row = row_of(x, y, z)
                for part, rows in enumerate((rows_re, rows_im)):
                    values = density_ref[part, x, y, z:z + 1, :]
                    rows[row:row + 1, :] = jnp.where(keep, values, 0.0)
    parts = (rows_re[...], rows_im[...])
    gap = jnp.zeros((32, 4), jnp.float32)
    columns = [
        [part[:, 0:64] for part in parts],
        [part[:, 232:296] for part in parts],
    ]
    for x in (1, 3, 5):
        pieces = []
        for part in parts:
            for layer in (x, x + 1):
                at = layer_start(layer)
                pieces += [part[:, at:at + 28], gap]
        columns.append(pieces)
    for place, pieces in enumerate(columns):
        out_ref[:, place * LANES:(place + 1) * LANES] = jnp.concatenate(pieces, axis=1)


def pack(occupied, density):
    width = density.shape[-1]
    return pl.pallas_call(
        pack_body,
        in_specs=[pl.BlockSpec(memory_space=pltpu.VMEM), pl.BlockSpec(memory_space=pltpu.VMEM)],
        out_specs=pl.BlockSpec(memory_space=pltpu.VMEM),
        out_shape=jax.ShapeDtypeStruct((32, COLUMNS * LANES), jnp.float32),
        scratch_shapes=[pltpu.VMEM((32, width), jnp.float32)] * 2,
        name="pack",
    )(occupied.transpose(0, 2, 1), density)


def unpack_body(occupied_ref, p0, p1, p2, p3, out_ref, rows_re, rows_im):
    values = (p0[...] + p1[...]) + (p2[...] + p3[...])
    for part, rows in enumerate((rows_re, rows_im)):
        base = 64 * part
        pieces = [values[:, base:base + 64]]
        for layer in range(6):
            at = (2 + layer // 2) * LANES + base + 32 * (layer % 2)
            pieces.append(values[:, at:at + 28])
        pieces.append(values[:, LANES + base:LANES + base + 64])
        rows[...] = jnp.concatenate(pieces, axis=1)
    for x in range(4):
        for y in range(4):
            for z in range(2):
                keep = occupied_ref[x, z:z + 1, y:y + 1] > 0
                row = row_of(x, y, z)
                for part, rows in enumerate((rows_re, rows_im)):
                    out_ref[part, x, y, z:z + 1, :] = jnp.where(keep, rows[row:row + 1, :], 0.0)


def unpack(occupied, parts, shape):
    in_vmem = pl.BlockSpec(memory_space=pltpu.VMEM)
    return pl.pallas_call(
        unpack_body,
        in_specs=[pl.BlockSpec(memory_space=pltpu.VMEM)] + [in_vmem] * 4,
        out_specs=in_vmem,
        out_shape=jax.ShapeDtypeStruct(shape, jnp.float32),
        scratch_shapes=[pltpu.VMEM((32, shape[-1]), jnp.float32)] * 2,
        name="unpack",
    )(occupied.transpose(0, 2, 1), *parts)


def split_bf16(values):
    high = values.astype(jnp.bfloat16)
    low = (values - high.astype(jnp.float32)).astype(jnp.bfloat16)
    return high, low


def translate_body(
    sub_count, freq_part,
    c0, c1, c2, c3, inner_ref, outer_ref, factor_ref, matrix_ref, table_ref, *refs,
):
    block_count = len(refs) - 4 - 13
    block_refs, (o0, o1, o2, o3) = refs[:block_count], refs[block_count:block_count + 4]
    (
        rows, rolled, layers, spectra, comps, sums, split_sums, moved, total, tables, pieces_in, kernel_ref, sem,
    ) = refs[block_count + 4:]
    slab, sub = lax.axis_index("slab"), lax.axis_index("sub")
    core = lax.rem(slab, 2)
    half_blocks = block_count // 2
    piece_count = LANES // freq_part
    class_count = tables.shape[0] // piece_count
    class_blocks = block_count // class_count
    plane = 4 * P_SIZE * P_SIZE

    variant = lax.div(lax.rem(freq_part * sub, plane), LANES) if table_ref.shape[0] > 1 else 0
    copy = pltpu.make_async_copy(table_ref.at[variant], tables, sem)
    copy.start()

    for k, chunk in enumerate((c0, c1, c2, c3)):
        source = sub ^ k
        for half in range(2):
            base = pl.multiple_of((2 * source + half) * 32, 32)
            rows[pl.ds(base + 8, 16), :] = chunk[half * 16:half * 16 + 16, :]
            at = k * 16 + half * 8
            rows[pl.ds(pl.multiple_of(base + 24 * (1 - core), 8), 8), :] = inner_ref[at:at + 8, :]
            rows[pl.ds(pl.multiple_of(base + 24 * core, 8), 8), :] = outer_ref[at:at + 8, :]
    for place in range(1, COLUMNS):
        lanes = slice(place * LANES, (place + 1) * LANES)
        for at in range(0, 256, 32):
            rolled[at:at + 32, lanes] = pltpu.roll(rows[at:at + 32, lanes], 64, 1)
    for at in range(0, comps.shape[0], 24):
        comps[at:at + 8, :] = jnp.zeros((8, LANES), jnp.float32)
        comps[at + 16:at + 24, :] = jnp.zeros((8, LANES), jnp.float32)
    total[...] = jnp.zeros_like(total)

    def split_store(ref, at, place, values):
        high, low = split_bf16(values)
        for third, piece in enumerate((high, low, high)):
            lanes = third * 256 + place * LANES
            ref[pl.ds(at, 16), lanes:lanes + LANES] = piece

    def factors(block, piece):
        odd = (block >= half_blocks).astype(jnp.int32)
        owner = slab ^ (2 * ((block - half_blocks * odd) * piece_count + piece) + odd)
        freq_x = lax.div(freq_part * (sub_count * owner + sub), plane)
        return [factor_ref[freq_x, row:row + 1, :] for row in range(8)]

    pieces_in[...] = jnp.zeros_like(pieces_in)

    for group in range(class_count):
        for piece in range(piece_count):

            def transform_x(index, _):
                factor = factors(group * class_blocks + index, piece)
                for at in range(0, 256, 16):
                    def column(ref, place):
                        return ref[at:at + 16, place * LANES:(place + 1) * LANES]

                    full = column(rows, 0) + (factor[0] * column(rows, 1) + factor[1] * column(rolled, 1))
                    ring = None
                    for pair in range(3):
                        term = (
                            factor[2 + 2 * pair] * column(rows, 2 + pair)
                            + factor[3 + 2 * pair] * column(rolled, 2 + pair)
                        )
                        ring = term if ring is None else ring + term
                    target = pl.multiple_of(index * 256 + at, 16)
                    split_store(layers, target, 0, full)
                    split_store(layers, target, 1, ring)
                return 0

            lax.fori_loop(0, class_blocks, transform_x, 0)
            if group == 0 and piece == 0:
                copy.wait()
            found = jnp.dot(layers[...], tables[group * piece_count + piece, 0], preferred_element_type=jnp.float32)
            span = slice(group * class_blocks * 256, (group + 1) * class_blocks * 256)
            for part in range(2):
                values = found[:, part * LANES:(part + 1) * LANES]
                if piece > 0:
                    values = values + spectra[part, span, :]
                spectra[part, span, :] = values

    for block in range(block_count):
        for part in range(2):
            left = block_refs[block][pl.ds(part, KEPT, stride=2), :]
            lanes = slice(part * LANES, (part + 1) * LANES)
            for turn in range(3):
                piece = left.astype(jnp.bfloat16)
                left = left - piece.astype(jnp.float32)
                pieces_in[block % 2, turn * KEPT_PADDED:turn * KEPT_PADDED + KEPT, lanes] = piece
        result = jnp.dot(matrix_ref[...], pieces_in[block % 2], preferred_element_type=jnp.float32)
        k_re, k_im = result[:, :LANES], result[:, LANES:]
        for part, value in enumerate((k_re, k_im - k_re, k_re + k_im)):
            kernel_ref[block, part] = value

    def translate_block(block):
        for parent in range(4):
            values = np.empty((2, 3, 3, 3), dtype=object)
            for part in range(2):
                for px in range(2):
                    for py in range(2):
                        for pz in range(2):
                            row = block * 256 + (2 * parent + px) * 4 + pz * 2 + py
                            values[part, px, py, pz] = spectra[part, pl.ds(row, 8, stride=32), :]
                for px in range(2):
                    for py in range(2):
                        values[part, px, py, 2] = values[part, px, py, 0] + values[part, px, py, 1]
                    for cz in range(3):
                        values[part, px, 2, cz] = values[part, px, 0, cz] + values[part, px, 1, cz]
                for cy in range(3):
                    for cz in range(3):
                        values[part, 2, cy, cz] = values[part, 0, cy, cz] + values[part, 1, cy, cz]
            for comp in range(27):
                for part in range(2):
                    value = values[part, comp // 9, comp // 3 % 3, comp % 3]
                    at = ((comp * 4 + parent) * 2 + part) * 24 + 8
                    comps[at:at + 8, :] = value

        def product(cx, cy, cz):
            comp = (cx * 3 + cy) * 3 + cz
            have = [[None] * 3 for _ in range(2)]
            for ey in (-1, 0, 1):
                source = []
                for parent in range(4):
                    at = (comp * 4 + parent) * 48 + 8 + ey
                    s_re, s_im = (comps[at + 24 * part:at + 24 * part + 8, :] for part in range(2))
                    source.append((s_re + s_im, s_re, s_im))
                for place, (ex, neighbour_y) in enumerate(NEIGHBOURS):
                    if neighbour_y != ey:
                        continue
                    row = comp * 8 + place
                    weights = [
                        jnp.broadcast_to(kernel_ref[block, part, row:row + 1, :], (8, LANES)) for part in range(3)
                    ]
                    for parent in range(2):
                        for part in range(3):
                            term = weights[part] * source[parent + 1 + ex][part]
                            old = have[parent][part]
                            have[parent][part] = term if old is None else old + term
            found = []
            for parent in range(2):
                first, second, third = have[parent]
                found += [first - third, first + second]
            return found

        def merge(low, high, both):
            return [b + h for b, h in zip(both, high)] + [b + l for b, l in zip(both, low)]

        def along_z(cx, cy):
            return merge(product(cx, cy, 0), product(cx, cy, 1), product(cx, cy, 2))

        def along_y(cx):
            return merge(along_z(cx, 0), along_z(cx, 1), along_z(cx, 2))

        values = merge(along_y(0), along_y(1), along_y(2))
        for px in range(2):
            for py in range(2):
                for pz in range(2):
                    for parent in range(2):
                        at = ((px * 2 + py) * 2 + pz) * 4 + parent * 2
                        row = (2 * parent + px) * 4 + pz * 2 + py
                        for part in range(2):
                            sums[part, pl.ds(row, 8, stride=16), :] = values[at + part]
        for at in range(0, 128, 16):
            for part in range(2):
                split_store(split_sums, pl.multiple_of(block * 128 + at, 16), part, sums[part, at:at + 16, :])

    def one_block(block, _):
        translate_block(block)
        return 0

    lax.fori_loop(0, block_count, one_block, 0)

    for group in range(class_count):
        span = slice(group * class_blocks * 128, (group + 1) * class_blocks * 128)
        for piece in range(piece_count):
            moved[...] = jnp.dot(split_sums[span, :], tables[group * piece_count + piece, 1], preferred_element_type=jnp.float32)

            def transform_back(index, _):
                factor = factors(group * class_blocks + index, piece)
                for at in range(0, 128, 16):
                    source = pl.ds(pl.multiple_of(index * 128 + at, 16), 16)
                    full, ring = moved[source, :LANES], moved[source, LANES:]
                    full_rolled, ring_rolled = pltpu.roll(full, 64, 1), pltpu.roll(ring, 64, 1)
                    total[at:at + 16, 0:LANES] += full
                    total[at:at + 16, LANES:2 * LANES] += factor[0] * full - factor[1] * full_rolled
                    for pair in range(3):
                        lanes = slice((2 + pair) * LANES, (3 + pair) * LANES)
                        total[at:at + 16, lanes] += (
                            factor[2 + 2 * pair] * ring - factor[3 + 2 * pair] * ring_rolled
                        )
                return 0

            lax.fori_loop(0, class_blocks, transform_back, 0)

    for k, out_ref in enumerate((o0, o1, o2, o3)):
        base = pl.multiple_of((sub ^ k) * 32, 32)
        out_ref[...] = total[pl.ds(base, 32), :] * (1.0 / 4096.0)


def translate(sub_count, freq_part, chunks, inner, outer, tables, blocks):
    block_count = len(blocks)
    class_blocks = block_count * (LANES // freq_part) // tables.shape[1]
    width = COLUMNS * LANES
    matrix = jnp.asarray(np.concatenate([expansion()] * 3, axis=1), jnp.bfloat16)
    f32, bf16 = jnp.float32, jnp.bfloat16
    in_vmem = pl.BlockSpec(memory_space=pltpu.VMEM)
    anywhere = pl.BlockSpec(memory_space=pl.ANY)
    return pl.pallas_call(
        functools.partial(translate_body, sub_count, freq_part),
        in_specs=[in_vmem] * 8 + [anywhere] + [in_vmem] * block_count,
        out_specs=[in_vmem] * 4,
        scratch_shapes=[
            pltpu.VMEM((256, width), f32),
            pltpu.VMEM((256, width), f32),
            pltpu.VMEM((class_blocks * 256, 768), bf16),
            pltpu.VMEM((2, block_count * 256, LANES), f32),
            pltpu.VMEM((4 * 54 * 24, LANES), f32),
            pltpu.VMEM((2, 128, LANES), f32),
            pltpu.VMEM((block_count * 128, 768), bf16),
            pltpu.VMEM((class_blocks * 128, 256), f32),
            pltpu.VMEM((128, width), f32),
            pltpu.VMEM(tables.shape[1:], bf16),
            pltpu.VMEM((2, 3 * KEPT_PADDED, 2 * LANES), bf16),
            pltpu.VMEM((block_count, 3, 27 * 8, LANES), f32),
            pltpu.SemaphoreType.DMA,
        ],
        out_shape=[jax.ShapeDtypeStruct((32, width), f32)] * 4,
        compiler_params=pltpu.CompilerParams(vmem_limit_bytes=VMEM_BYTES),
        name="translate",
    )(*chunks, inner, outer, jnp.asarray(layer_factors()), matrix, tables, *blocks)


def plane_layout():
    points = surface_points(P_SIZE)
    layer = points[1:, points[0] == 1]
    at_y, at_z, used, part = (np.zeros(256, np.int32) for _ in range(4))
    at_y[:128], at_z[:128] = np.arange(128) % 64 // 8, np.arange(128) % 8
    used[:128], part[:128] = 1, np.arange(128) // 64
    for half in range(2):
        for slot in range(2):
            base = 128 + 64 * half + 32 * slot
            at_y[base:base + 28], at_z[base:base + 28] = layer
            used[base:base + 28], part[base:base + 28] = 1, half
    return at_y, at_z, used, part


def plane_tables(freq, freq_part):
    side = 2 * P_SIZE
    at_y, at_z, used, part = plane_layout()
    lib = np if isinstance(freq, np.ndarray) else jnp
    freq_y, freq_z = freq // side % side, freq % side
    column = lambda values: values[None, :, None]
    turns = column(at_y) * freq_y[:, None, :] + column(at_z) * freq_z[:, None, :]
    quarter = side // 4
    turns = lib.concatenate([turns - quarter * column(part), turns + quarter * column(1 - part)], axis=2)
    values = lib.cos((turns % side).astype(np.float32) * np.float32(2.0 * math.pi / side)) * column(used.astype(np.float32))
    pieces = LANES // freq_part
    owner = np.arange(2 * LANES) % LANES // freq_part
    mine = (owner[None, :] == np.arange(pieces)[:, None]).astype(np.float32)
    values = (values[:, None] * mine[None, :, None, :]).reshape(-1, 256, 256)
    if lib is np:
        high = values.astype(jnp.bfloat16).astype(np.float32)
    else:
        high = lax.reduce_precision(values, 8, 7)
    low = values - high
    both = []
    for turned in (False, True):
        third = [lib.swapaxes(piece, 1, 2) if turned else piece for piece in (high, high, low)]
        both.append(lib.concatenate(third, axis=1))
    return lib.stack(both, axis=1).astype(jnp.bfloat16)


def layer_factors():
    side = 2 * P_SIZE
    lane = np.arange(LANES)
    layer = np.stack([np.full(LANES, 7)] + [2 * pair + 1 + lane % 64 // 32 for pair in range(3)])
    sign = np.where(lane < 64, 1.0, -1.0)
    angles = (layer[None] * np.arange(side)[:, None, None] % side) * (2.0 * math.pi / side)
    both = np.stack([np.cos(angles), np.sin(angles) * sign], axis=2)
    return both.reshape(side, 8, LANES).astype(np.float32)


def local(density, occupied, kernels):
    block_x, block_y, block_z, surf_count = density.shape[1:]
    slab_count = lax.axis_size("slab")
    sub_count = lax.axis_size("sub")
    freq_part = kernels.shape[-1]
    assert (block_x, block_y, block_z, sub_count) == (4, 4, 2, 4)
    slab, sub = lax.axis_index("slab"), lax.axis_index("sub")
    core = slab % 2

    def exchange(values, axis, bits):
        pairs = [(i, i ^ bits) for i in range(lax.axis_size(axis))]
        return lax.ppermute(values, axis, pairs)

    own, mine = pack(occupied, density), compact_kernels(kernels)
    width = own.shape[-1]
    chunks = [own] + [exchange(own, "sub", k) for k in range(1, 4)]

    same_core = [mine] + [exchange(mine, "slab", m) for m in range(2, slab_count, 2)]

    def rows_at(start):
        parts = [lax.dynamic_slice_in_dim(chunk.reshape(2, 16, width), start, 8, 1) for chunk in chunks]
        return jnp.concatenate(parts).reshape(64, width)

    across = [(i, i + 1) for i in range(1, slab_count - 1, 2)]
    across += [(right, left) for left, right in across]
    outer, inner = rows_at(8 * core), rows_at(8 * (1 - core))
    outer, inner, same_core = lax.optimization_barrier((outer, inner, same_core))
    outer = lax.ppermute(outer, "slab", across)
    inner = exchange(inner, "slab", 1)

    other_core = [exchange(block, "slab", 1) for block in same_core]
    pieces = LANES // freq_part
    block_count = slab_count // pieces

    def by_block(blocks):
        return [jnp.concatenate(blocks[at:at + pieces], axis=1) for at in range(0, len(blocks), pieces)]

    blocks = same_core + other_core if pieces == 1 else by_block(same_core) + by_block(other_core)
    plane = 4 * P_SIZE * P_SIZE
    if pieces == 1 and (freq_part * sub_count) % plane == 0:
        freq = np.arange(plane, dtype=np.int32).reshape(-1, LANES)
        tables = jnp.asarray(plane_tables(freq, freq_part))[:, None]
    else:
        owner = slab ^ jnp.asarray([2 * k + half for half in range(2) for k in range(pieces)], jnp.int32)
        base = freq_part * (sub_count * owner + sub)
        freq = (base[:, None] + jnp.arange(freq_part)[None, :]).reshape(2, LANES).astype(jnp.int32)
        tables = plane_tables(freq, freq_part)[None]

    parts = translate(sub_count, freq_part, chunks, inner, outer, tables, blocks)
    fields = [parts[0]] + [exchange(parts[k], "sub", k) for k in (3, 2, 1)]
    return unpack(occupied, fields, density.shape)


def solution(mesh):
    return jax.shard_map(
        local,
        mesh=mesh,
        in_specs=(
            P(None, "slab", "sub", None, None),
            P("slab", "sub", None),
            P(None, None, ("slab", "sub")),
        ),
        out_specs=P(None, "slab", "sub", None, None),
        check_vma=False,
    )
```

```python
import functools
import math

import jax
import jax.numpy as jnp
import numpy as np
from jax import lax
from jax.experimental import pallas as pl
from jax.experimental.pallas import tpu as pltpu
from jax.sharding import PartitionSpec as P

P_SIZE = 8
LANES = 128
COLUMNS = 5
VMEM_BYTES = 56 * 1024 * 1024
NEIGHBOURS = [(ex, ey) for ex in (-1, 0, 1) for ey in (-1, 0, 1) if (ex, ey) != (0, 0)]


def surface_points(edge_count):
    rows_found = []
    for first in range(edge_count):
        for second in range(edge_count):
            for third in range(edge_count):
                if min(first, second, third) == 0 or max(first, second, third) == edge_count - 1:
                    rows_found.append((first, second, third))
    return np.array(rows_found, dtype=np.int32).T


def offset_slots():
    slots = {}
    for step_x in range(-3, 4):
        for step_y in range(-3, 4):
            for step_z in range(-3, 4):
                if max(abs(step_x), abs(step_y), abs(step_z)) > 1:
                    slots[step_x, step_y, step_z] = len(slots)
    return slots


def column_groups():
    slots = offset_slots()
    return {key[:2]: slot for key, slot in slots.items() if key[2] == -1}


GROUPS = column_groups()
GROUP_ROW = {key: 3 * place for place, key in enumerate(GROUPS)}
KEPT = 3 * len(GROUPS)
KEPT_PADDED = 128


def expansion():
    weights = ((1, -1, 0), (0, -1, 1), (0, 1, 0))
    found = np.zeros((27 * 8, KEPT_PADDED), np.float32)
    for comp in range(27):
        cx, cy, cz = comp // 9, comp // 3 % 3, comp % 3
        for place, (ex, ey) in enumerate(NEIGHBOURS):
            for ax in range(3):
                for ay in range(3):
                    row = GROUP_ROW.get((2 * ex + ax - 1, 2 * ey + ay - 1))
                    if row is not None:
                        for az in range(3):
                            found[comp * 8 + place, row + az] += weights[cx][ax] * weights[cy][ay] * weights[cz][az]
    return found


def compact_body(kernel_ref, out_ref, held, sem):
    copy = pltpu.make_async_copy(kernel_ref, held, sem)
    copy.start()
    copy.wait()
    for key, slot in GROUPS.items():
        row = 2 * GROUP_ROW[key]
        out_ref[row:row + 6, :] = held[2 * slot:2 * slot + 6, :]


def compact_kernels(kernels):
    rows, width = kernels.shape[1:]
    return pl.pallas_call(
        compact_body,
        in_specs=[pl.BlockSpec(memory_space=pl.ANY)],
        out_specs=pl.BlockSpec(memory_space=pltpu.VMEM),
        out_shape=jax.ShapeDtypeStruct((2 * KEPT, width), jnp.float32),
        scratch_shapes=[pltpu.VMEM((2 * rows, width), jnp.float32), pltpu.SemaphoreType.DMA],
        name="compact",
    )(kernels.transpose(1, 0, 2).reshape(2 * rows, width))


def row_of(x, y, z):
    return (y // 2) * 16 + x * 4 + z * 2 + y % 2


def layer_start(x):
    return 64 + 28 * (x - 1)


def pack_body(occupied_ref, density_ref, out_ref, rows_re, rows_im):
    for x in range(4):
        for y in range(4):
            for z in range(2):
                keep = occupied_ref[x, z:z + 1, y:y + 1] > 0
                row = row_of(x, y, z)
                for part, rows in enumerate((rows_re, rows_im)):
                    values = density_ref[part, x, y, z:z + 1, :]
                    rows[row:row + 1, :] = jnp.where(keep, values, 0.0)
    parts = (rows_re[...], rows_im[...])
    gap = jnp.zeros((32, 4), jnp.float32)
    columns = [
        [part[:, 0:64] for part in parts],
        [part[:, 232:296] for part in parts],
    ]
    for x in (1, 3, 5):
        pieces = []
        for part in parts:
            for layer in (x, x + 1):
                at = layer_start(layer)
                pieces += [part[:, at:at + 28], gap]
        columns.append(pieces)
    for place, pieces in enumerate(columns):
        out_ref[:, place * LANES:(place + 1) * LANES] = jnp.concatenate(pieces, axis=1)


def pack(occupied, density):
    width = density.shape[-1]
    return pl.pallas_call(
        pack_body,
        in_specs=[pl.BlockSpec(memory_space=pltpu.VMEM), pl.BlockSpec(memory_space=pltpu.VMEM)],
        out_specs=pl.BlockSpec(memory_space=pltpu.VMEM),
        out_shape=jax.ShapeDtypeStruct((32, COLUMNS * LANES), jnp.float32),
        scratch_shapes=[pltpu.VMEM((32, width), jnp.float32)] * 2,
        name="pack",
    )(occupied.transpose(0, 2, 1), density)


def unpack_body(occupied_ref, p0, p1, p2, p3, out_ref, rows_re, rows_im):
    values = (p0[...] + p1[...]) + (p2[...] + p3[...])
    for part, rows in enumerate((rows_re, rows_im)):
        base = 64 * part
        pieces = [values[:, base:base + 64]]
        for layer in range(6):
            at = (2 + layer // 2) * LANES + base + 32 * (layer % 2)
            pieces.append(values[:, at:at + 28])
        pieces.append(values[:, LANES + base:LANES + base + 64])
        rows[...] = jnp.concatenate(pieces, axis=1)
    for x in range(4):
        for y in range(4):
            for z in range(2):
                keep = occupied_ref[x, z:z + 1, y:y + 1] > 0
                row = row_of(x, y, z)
                for part, rows in enumerate((rows_re, rows_im)):
                    out_ref[part, x, y, z:z + 1, :] = jnp.where(keep, rows[row:row + 1, :], 0.0)


def unpack(occupied, parts, shape):
    in_vmem = pl.BlockSpec(memory_space=pltpu.VMEM)
    return pl.pallas_call(
        unpack_body,
        in_specs=[pl.BlockSpec(memory_space=pltpu.VMEM)] + [in_vmem] * 4,
        out_specs=in_vmem,
        out_shape=jax.ShapeDtypeStruct(shape, jnp.float32),
        scratch_shapes=[pltpu.VMEM((32, shape[-1]), jnp.float32)] * 2,
        name="unpack",
    )(occupied.transpose(0, 2, 1), *parts)


def split_bf16(values):
    high = values.astype(jnp.bfloat16)
    low = (values - high.astype(jnp.float32)).astype(jnp.bfloat16)
    return high, low


def translate_body(
    sub_count, freq_part,
    c0, c1, c2, c3, inner_ref, outer_ref, factor_ref, matrix_ref, table_ref, *refs,
):
    block_count = len(refs) - 4 - 13
    block_refs, (o0, o1, o2, o3) = refs[:block_count], refs[block_count:block_count + 4]
    (
        rows, rolled, layers, spectra, comps, sums, split_sums, moved, total, tables, pieces_in, kernel_ref, sem,
    ) = refs[block_count + 4:]
    slab, sub = lax.axis_index("slab"), lax.axis_index("sub")
    core = lax.rem(slab, 2)
    half_blocks = block_count // 2
    piece_count = LANES // freq_part
    class_count = tables.shape[0] // piece_count
    class_blocks = block_count // class_count
    plane = 4 * P_SIZE * P_SIZE

    variant = lax.div(lax.rem(freq_part * sub, plane), LANES) if table_ref.shape[0] > 1 else 0
    copy = pltpu.make_async_copy(table_ref.at[variant], tables, sem)
    copy.start()

    for k, chunk in enumerate((c0, c1, c2, c3)):
        source = sub ^ k
        for half in range(2):
            base = pl.multiple_of((2 * source + half) * 32, 32)
            rows[pl.ds(base + 8, 16), :] = chunk[half * 16:half * 16 + 16, :]
            at = k * 16 + half * 8
            rows[pl.ds(pl.multiple_of(base + 24 * (1 - core), 8), 8), :] = inner_ref[at:at + 8, :]
            rows[pl.ds(pl.multiple_of(base + 24 * core, 8), 8), :] = outer_ref[at:at + 8, :]
    for place in range(1, COLUMNS):
        lanes = slice(place * LANES, (place + 1) * LANES)
        for at in range(0, 256, 32):
            rolled[at:at + 32, lanes] = pltpu.roll(rows[at:at + 32, lanes], 64, 1)
    for at in range(0, comps.shape[0], 24):
        comps[at:at + 8, :] = jnp.zeros((8, LANES), jnp.float32)
        comps[at + 16:at + 24, :] = jnp.zeros((8, LANES), jnp.float32)
    total[...] = jnp.zeros_like(total)

    def split_store(ref, at, place, values):
        high, low = split_bf16(values)
        for third, piece in enumerate((high, low, high)):
            lanes = third * 256 + place * LANES
            ref[pl.ds(at, 16), lanes:lanes + LANES] = piece

    def factors(block, piece):
        odd = (block >= half_blocks).astype(jnp.int32)
        owner = slab ^ (2 * ((block - half_blocks * odd) * piece_count + piece) + odd)
        freq_x = lax.div(freq_part * (sub_count * owner + sub), plane)
        return [factor_ref[freq_x, row:row + 1, :] for row in range(8)]

    pieces_in[...] = jnp.zeros_like(pieces_in)

    for group in range(class_count):
        for piece in range(piece_count):

            def transform_x(index, _):
                factor = factors(group * class_blocks + index, piece)
                for at in range(0, 256, 16):
                    def column(ref, place):
                        return ref[at:at + 16, place * LANES:(place + 1) * LANES]

                    full = column(rows, 0) + (factor[0] * column(rows, 1) + factor[1] * column(rolled, 1))
                    ring = None
                    for pair in range(3):
                        term = (
                            factor[2 + 2 * pair] * column(rows, 2 + pair)
                            + factor[3 + 2 * pair] * column(rolled, 2 + pair)
                        )
                        ring = term if ring is None else ring + term
                    target = pl.multiple_of(index * 256 + at, 16)
                    split_store(layers, target, 0, full)
                    split_store(layers, target, 1, ring)
                return 0

            lax.fori_loop(0, class_blocks, transform_x, 0)
            if group == 0 and piece == 0:
                copy.wait()
            found = jnp.dot(layers[...], tables[group * piece_count + piece, 0], preferred_element_type=jnp.float32)
            span = slice(group * class_blocks * 256, (group + 1) * class_blocks * 256)
            for part in range(2):
                values = found[:, part * LANES:(part + 1) * LANES]
                if piece > 0:
                    values = values + spectra[part, span, :]
                spectra[part, span, :] = values

    for block in range(block_count):
        for part in range(2):
            left = block_refs[block][pl.ds(part, KEPT, stride=2), :]
            lanes = slice(part * LANES, (part + 1) * LANES)
            for turn in range(3):
                piece = left.astype(jnp.bfloat16)
                left = left - piece.astype(jnp.float32)
                pieces_in[block % 2, turn * KEPT_PADDED:turn * KEPT_PADDED + KEPT, lanes] = piece
        result = jnp.dot(matrix_ref[...], pieces_in[block % 2], preferred_element_type=jnp.float32)
        k_re, k_im = result[:, :LANES], result[:, LANES:]
        for part, value in enumerate((k_re, k_im - k_re, k_re + k_im)):
            kernel_ref[block, part] = value

    def translate_block(block):
        for parent in range(4):
            values = np.empty((2, 3, 3, 3), dtype=object)
            for part in range(2):
                for px in range(2):
                    for py in range(2):
                        for pz in range(2):
                            row = block * 256 + (2 * parent + px) * 4 + pz * 2 + py
                            values[part, px, py, pz] = spectra[part, pl.ds(row, 8, stride=32), :]
                for px in range(2):
                    for py in range(2):
                        values[part, px, py, 2] = values[part, px, py, 0] + values[part, px, py, 1]
                    for cz in range(3):
                        values[part, px, 2, cz] = values[part, px, 0, cz] + values[part, px, 1, cz]
                for cy in range(3):
                    for cz in range(3):
                        values[part, 2, cy, cz] = values[part, 0, cy, cz] + values[part, 1, cy, cz]
            for comp in range(27):
                for part in range(2):
                    value = values[part, comp // 9, comp // 3 % 3, comp % 3]
                    at = ((comp * 4 + parent) * 2 + part) * 24 + 8
                    comps[at:at + 8, :] = value

        def product(cx, cy, cz):
            comp = (cx * 3 + cy) * 3 + cz
            have = [[None] * 3 for _ in range(2)]
            for ey in (-1, 0, 1):
                source = []
                for parent in range(4):
                    at = (comp * 4 + parent) * 48 + 8 + ey
                    s_re, s_im = (comps[at + 24 * part:at + 24 * part + 8, :] for part in range(2))
                    source.append((s_re + s_im, s_re, s_im))
                for place, (ex, neighbour_y) in enumerate(NEIGHBOURS):
                    if neighbour_y != ey:
                        continue
                    row = comp * 8 + place
                    weights = [
                        jnp.broadcast_to(kernel_ref[block, part, row:row + 1, :], (8, LANES)) for part in range(3)
                    ]
                    for parent in range(2):
                        for part in range(3):
                            term = weights[part] * source[parent + 1 + ex][part]
                            old = have[parent][part]
                            have[parent][part] = term if old is None else old + term
            found = []
            for parent in range(2):
                first, second, third = have[parent]
                found += [first - third, first + second]
            return found

        def merge(low, high, both):
            return [b + h for b, h in zip(both, high)] + [b + l for b, l in zip(both, low)]

        def along_z(cx, cy):
            return merge(product(cx, cy, 0), product(cx, cy, 1), product(cx, cy, 2))

        def along_y(cx):
            return merge(along_z(cx, 0), along_z(cx, 1), along_z(cx, 2))

        values = merge(along_y(0), along_y(1), along_y(2))
        for px in range(2):
            for py in range(2):
                for pz in range(2):
                    for parent in range(2):
                        at = ((px * 2 + py) * 2 + pz) * 4 + parent * 2
                        row = (2 * parent + px) * 4 + pz * 2 + py
                        for part in range(2):
                            sums[part, pl.ds(row, 8, stride=16), :] = values[at + part]
        for at in range(0, 128, 16):
            for part in range(2):
                split_store(split_sums, pl.multiple_of(block * 128 + at, 16), part, sums[part, at:at + 16, :])

    def one_block(block, _):
        translate_block(block)
        return 0

    lax.fori_loop(0, block_count, one_block, 0)

    for group in range(class_count):
        span = slice(group * class_blocks * 128, (group + 1) * class_blocks * 128)
        for piece in range(piece_count):
            moved[...] = jnp.dot(split_sums[span, :], tables[group * piece_count + piece, 1], preferred_element_type=jnp.float32)

            def transform_back(index, _):
                factor = factors(group * class_blocks + index, piece)
                for at in range(0, 128, 16):
                    source = pl.ds(pl.multiple_of(index * 128 + at, 16), 16)
                    full, ring = moved[source, :LANES], moved[source, LANES:]
                    full_rolled, ring_rolled = pltpu.roll(full, 64, 1), pltpu.roll(ring, 64, 1)
                    total[at:at + 16, 0:LANES] += full
                    total[at:at + 16, LANES:2 * LANES] += factor[0] * full - factor[1] * full_rolled
                    for pair in range(3):
                        lanes = slice((2 + pair) * LANES, (3 + pair) * LANES)
                        total[at:at + 16, lanes] += (
                            factor[2 + 2 * pair] * ring - factor[3 + 2 * pair] * ring_rolled
                        )
                return 0

            lax.fori_loop(0, class_blocks, transform_back, 0)

    for k, out_ref in enumerate((o0, o1, o2, o3)):
        base = pl.multiple_of((sub ^ k) * 32, 32)
        out_ref[...] = total[pl.ds(base, 32), :] * (1.0 / 4096.0)


def translate(sub_count, freq_part, chunks, inner, outer, tables, blocks):
    block_count = len(blocks)
    class_blocks = block_count * (LANES // freq_part) // tables.shape[1]
    width = COLUMNS * LANES
    matrix = jnp.asarray(np.concatenate([expansion()] * 3, axis=1), jnp.bfloat16)
    f32, bf16 = jnp.float32, jnp.bfloat16
    in_vmem = pl.BlockSpec(memory_space=pltpu.VMEM)
    anywhere = pl.BlockSpec(memory_space=pl.ANY)
    return pl.pallas_call(
        functools.partial(translate_body, sub_count, freq_part),
        in_specs=[in_vmem] * 8 + [anywhere] + [in_vmem] * block_count,
        out_specs=[in_vmem] * 4,
        scratch_shapes=[
            pltpu.VMEM((256, width), f32),
            pltpu.VMEM((256, width), f32),
            pltpu.VMEM((class_blocks * 256, 768), bf16),
            pltpu.VMEM((2, block_count * 256, LANES), f32),
            pltpu.VMEM((4 * 54 * 24, LANES), f32),
            pltpu.VMEM((2, 128, LANES), f32),
            pltpu.VMEM((block_count * 128, 768), bf16),
            pltpu.VMEM((class_blocks * 128, 256), f32),
            pltpu.VMEM((128, width), f32),
            pltpu.VMEM(tables.shape[1:], bf16),
            pltpu.VMEM((2, 3 * KEPT_PADDED, 2 * LANES), bf16),
            pltpu.VMEM((block_count, 3, 27 * 8, LANES), f32),
            pltpu.SemaphoreType.DMA,
        ],
        out_shape=[jax.ShapeDtypeStruct((32, width), f32)] * 4,
        compiler_params=pltpu.CompilerParams(vmem_limit_bytes=VMEM_BYTES),
        name="translate",
    )(*chunks, inner, outer, jnp.asarray(layer_factors()), matrix, tables, *blocks)


def plane_layout():
    points = surface_points(P_SIZE)
    layer = points[1:, points[0] == 1]
    at_y, at_z, used, part = (np.zeros(256, np.int32) for _ in range(4))
    at_y[:128], at_z[:128] = np.arange(128) % 64 // 8, np.arange(128) % 8
    used[:128], part[:128] = 1, np.arange(128) // 64
    for half in range(2):
        for slot in range(2):
            base = 128 + 64 * half + 32 * slot
            at_y[base:base + 28], at_z[base:base + 28] = layer
            used[base:base + 28], part[base:base + 28] = 1, half
    return at_y, at_z, used, part


def plane_tables(freq, freq_part):
    side = 2 * P_SIZE
    at_y, at_z, used, part = plane_layout()
    lib = np if isinstance(freq, np.ndarray) else jnp
    freq_y, freq_z = freq // side % side, freq % side
    column = lambda values: values[None, :, None]
    turns = column(at_y) * freq_y[:, None, :] + column(at_z) * freq_z[:, None, :]
    quarter = side // 4
    turns = lib.concatenate([turns - quarter * column(part), turns + quarter * column(1 - part)], axis=2)
    values = lib.cos((turns % side).astype(np.float32) * np.float32(2.0 * math.pi / side)) * column(used.astype(np.float32))
    pieces = LANES // freq_part
    owner = np.arange(2 * LANES) % LANES // freq_part
    mine = (owner[None, :] == np.arange(pieces)[:, None]).astype(np.float32)
    values = (values[:, None] * mine[None, :, None, :]).reshape(-1, 256, 256)
    if lib is np:
        high = values.astype(jnp.bfloat16).astype(np.float32)
    else:
        high = lax.reduce_precision(values, 8, 7)
    low = values - high
    both = []
    for turned in (False, True):
        third = [lib.swapaxes(piece, 1, 2) if turned else piece for piece in (high, high, low)]
        both.append(lib.concatenate(third, axis=1))
    return lib.stack(both, axis=1).astype(jnp.bfloat16)


def layer_factors():
    side = 2 * P_SIZE
    lane = np.arange(LANES)
    layer = np.stack([np.full(LANES, 7)] + [2 * pair + 1 + lane % 64 // 32 for pair in range(3)])
    sign = np.where(lane < 64, 1.0, -1.0)
    angles = (layer[None] * np.arange(side)[:, None, None] % side) * (2.0 * math.pi / side)
    both = np.stack([np.cos(angles), np.sin(angles) * sign], axis=2)
    return both.reshape(side, 8, LANES).astype(np.float32)


def local(density, occupied, kernels):
    block_x, block_y, block_z, surf_count = density.shape[1:]
    slab_count = lax.axis_size("slab")
    sub_count = lax.axis_size("sub")
    freq_part = kernels.shape[-1]
    assert (block_x, block_y, block_z, sub_count) == (4, 4, 2, 4)
    slab, sub = lax.axis_index("slab"), lax.axis_index("sub")
    core = slab % 2

    def exchange(values, axis, bits):
        pairs = [(i, i ^ bits) for i in range(lax.axis_size(axis))]
        return lax.ppermute(values, axis, pairs)

    own, mine = pack(occupied, density), compact_kernels(kernels)
    width = own.shape[-1]
    chunks = [own] + [exchange(own, "sub", k) for k in range(1, 4)]

    same_core = [mine] + [exchange(mine, "slab", m) for m in range(2, slab_count, 2)]

    def rows_at(start):
        parts = [lax.dynamic_slice_in_dim(chunk.reshape(2, 16, width), start, 8, 1) for chunk in chunks]
        return jnp.concatenate(parts).reshape(64, width)

    across = [(i, i + 1) for i in range(1, slab_count - 1, 2)]
    across += [(right, left) for left, right in across]
    outer, inner = rows_at(8 * core), rows_at(8 * (1 - core))
    sibling = exchange(mine, "slab", 1)
    _, _, same_core, sibling = lax.optimization_barrier((outer, inner, same_core, sibling))
    outer = lax.ppermute(outer, "slab", across)
    inner = exchange(inner, "slab", 1)

    other_core = [sibling] + [exchange(block, "slab", 1) for block in same_core[1:]]
    pieces = LANES // freq_part
    block_count = slab_count // pieces

    def by_block(blocks):
        return [jnp.concatenate(blocks[at:at + pieces], axis=1) for at in range(0, len(blocks), pieces)]

    blocks = same_core + other_core if pieces == 1 else by_block(same_core) + by_block(other_core)
    plane = 4 * P_SIZE * P_SIZE
    if pieces == 1 and (freq_part * sub_count) % plane == 0:
        freq = np.arange(plane, dtype=np.int32).reshape(-1, LANES)
        tables = jnp.asarray(plane_tables(freq, freq_part))[:, None]
    else:
        owner = slab ^ jnp.asarray([2 * k + half for half in range(2) for k in range(pieces)], jnp.int32)
        base = freq_part * (sub_count * owner + sub)
        freq = (base[:, None] + jnp.arange(freq_part)[None, :]).reshape(2, LANES).astype(jnp.int32)
        tables = plane_tables(freq, freq_part)[None]

    parts = translate(sub_count, freq_part, chunks, inner, outer, tables, blocks)
    fields = [parts[0]] + [exchange(parts[k], "sub", k) for k in (3, 2, 1)]
    return unpack(occupied, fields, density.shape)


def solution(mesh):
    return jax.shard_map(
        local,
        mesh=mesh,
        in_specs=(
            P(None, "slab", "sub", None, None),
            P("slab", "sub", None),
            P(None, None, ("slab", "sub")),
        ),
        out_specs=P(None, "slab", "sub", None, None),
        check_vma=False,
    )
```

```python
import functools
import math

import jax
import jax.numpy as jnp
import numpy as np
from jax import lax
from jax.experimental import pallas as pl
from jax.experimental.pallas import tpu as pltpu
from jax.sharding import PartitionSpec as P

P_SIZE = 8
LANES = 128
COLUMNS = 5
VMEM_BYTES = 56 * 1024 * 1024
NEIGHBOURS = [(ex, ey) for ex in (-1, 0, 1) for ey in (-1, 0, 1) if (ex, ey) != (0, 0)]


def surface_points(edge_count):
    rows_found = []
    for first in range(edge_count):
        for second in range(edge_count):
            for third in range(edge_count):
                if min(first, second, third) == 0 or max(first, second, third) == edge_count - 1:
                    rows_found.append((first, second, third))
    return np.array(rows_found, dtype=np.int32).T


def offset_slots():
    slots = {}
    for step_x in range(-3, 4):
        for step_y in range(-3, 4):
            for step_z in range(-3, 4):
                if max(abs(step_x), abs(step_y), abs(step_z)) > 1:
                    slots[step_x, step_y, step_z] = len(slots)
    return slots


def column_groups():
    slots = offset_slots()
    return {key[:2]: slot for key, slot in slots.items() if key[2] == -1}


GROUPS = column_groups()
GROUP_ROW = {key: 3 * place for place, key in enumerate(GROUPS)}
KEPT = 3 * len(GROUPS)
KEPT_PADDED = 128


def expansion():
    weights = ((1, -1, 0), (0, -1, 1), (0, 1, 0))
    found = np.zeros((27 * 8, KEPT_PADDED), np.float32)
    for comp in range(27):
        cx, cy, cz = comp // 9, comp // 3 % 3, comp % 3
        for place, (ex, ey) in enumerate(NEIGHBOURS):
            for ax in range(3):
                for ay in range(3):
                    row = GROUP_ROW.get((2 * ex + ax - 1, 2 * ey + ay - 1))
                    if row is not None:
                        for az in range(3):
                            found[comp * 8 + place, row + az] += weights[cx][ax] * weights[cy][ay] * weights[cz][az]
    return found


def row_of(x, y, z):
    return (y // 2) * 16 + x * 4 + z * 2 + y % 2


def layer_start(x):
    return 64 + 28 * (x - 1)


def prepare_body(occupied_ref, density_ref, kernel_ref, own_ref, kept_ref, density, kernels, rows_re, rows_im, sems):
    copies = [
        pltpu.make_async_copy(density_ref, density, sems.at[0]),
        pltpu.make_async_copy(kernel_ref, kernels, sems.at[1]),
    ]
    for copy in copies:
        copy.start()
    copies[0].wait()
    for x in range(4):
        for y in range(4):
            for z in range(2):
                keep = occupied_ref[x, z:z + 1, y:y + 1] > 0
                row = row_of(x, y, z)
                for part, rows in enumerate((rows_re, rows_im)):
                    values = density[part, x, y, z:z + 1, :]
                    rows[row:row + 1, :] = jnp.where(keep, values, 0.0)
    parts = (rows_re[...], rows_im[...])
    gap = jnp.zeros((32, 4), jnp.float32)
    columns = [
        [part[:, 0:64] for part in parts],
        [part[:, 232:296] for part in parts],
    ]
    for x in (1, 3, 5):
        pieces = []
        for part in parts:
            for layer in (x, x + 1):
                at = layer_start(layer)
                pieces += [part[:, at:at + 28], gap]
        columns.append(pieces)
    for place, pieces in enumerate(columns):
        own_ref[:, place * LANES:(place + 1) * LANES] = jnp.concatenate(pieces, axis=1)
    copies[1].wait()
    for key, slot in GROUPS.items():
        row = 2 * GROUP_ROW[key]
        kept_ref[row:row + 6, :] = kernels[2 * slot:2 * slot + 6, :]


def prepare(occupied, density, kernels):
    rows, width = 2 * kernels.shape[1], kernels.shape[2]
    surf_count = density.shape[-1]
    f32 = jnp.float32
    in_vmem = pl.BlockSpec(memory_space=pltpu.VMEM)
    anywhere = pl.BlockSpec(memory_space=pl.ANY)
    return pl.pallas_call(
        prepare_body,
        in_specs=[in_vmem, anywhere, anywhere],
        out_specs=[in_vmem] * 2,
        out_shape=[
            jax.ShapeDtypeStruct((32, COLUMNS * LANES), f32),
            jax.ShapeDtypeStruct((2 * KEPT, width), f32),
        ],
        scratch_shapes=[
            pltpu.VMEM(density.shape, f32),
            pltpu.VMEM((rows, width), f32),
            pltpu.VMEM((32, surf_count), f32),
            pltpu.VMEM((32, surf_count), f32),
            pltpu.SemaphoreType.DMA((2,)),
        ],
        name="prepare",
    )(occupied.transpose(0, 2, 1), density, kernels.transpose(1, 0, 2).reshape(rows, width))


def unpack_body(occupied_ref, p0, p1, p2, p3, out_ref, rows_re, rows_im):
    values = (p0[...] + p1[...]) + (p2[...] + p3[...])
    for part, rows in enumerate((rows_re, rows_im)):
        base = 64 * part
        pieces = [values[:, base:base + 64]]
        for layer in range(6):
            at = (2 + layer // 2) * LANES + base + 32 * (layer % 2)
            pieces.append(values[:, at:at + 28])
        pieces.append(values[:, LANES + base:LANES + base + 64])
        rows[...] = jnp.concatenate(pieces, axis=1)
    for x in range(4):
        for y in range(4):
            for z in range(2):
                keep = occupied_ref[x, z:z + 1, y:y + 1] > 0
                row = row_of(x, y, z)
                for part, rows in enumerate((rows_re, rows_im)):
                    out_ref[part, x, y, z:z + 1, :] = jnp.where(keep, rows[row:row + 1, :], 0.0)


def unpack(occupied, parts, shape):
    in_vmem = pl.BlockSpec(memory_space=pltpu.VMEM)
    return pl.pallas_call(
        unpack_body,
        in_specs=[pl.BlockSpec(memory_space=pltpu.VMEM)] + [in_vmem] * 4,
        out_specs=in_vmem,
        out_shape=jax.ShapeDtypeStruct(shape, jnp.float32),
        scratch_shapes=[pltpu.VMEM((32, shape[-1]), jnp.float32)] * 2,
        name="unpack",
    )(occupied.transpose(0, 2, 1), *parts)


def split_bf16(values):
    high = values.astype(jnp.bfloat16)
    low = (values - high.astype(jnp.float32)).astype(jnp.bfloat16)
    return high, low


def translate_body(
    sub_count, freq_part,
    c0, c1, c2, c3, inner_ref, outer_ref, factor_ref, matrix_ref, table_ref, *refs,
):
    block_count = len(refs) - 4 - 13
    block_refs, (o0, o1, o2, o3) = refs[:block_count], refs[block_count:block_count + 4]
    (
        rows, rolled, layers, spectra, comps, sums, split_sums, moved, total, tables, pieces_in, kernel_ref, sem,
    ) = refs[block_count + 4:]
    slab, sub = lax.axis_index("slab"), lax.axis_index("sub")
    core = lax.rem(slab, 2)
    half_blocks = block_count // 2
    piece_count = LANES // freq_part
    class_count = tables.shape[0] // piece_count
    class_blocks = block_count // class_count
    plane = 4 * P_SIZE * P_SIZE

    variant = lax.div(lax.rem(freq_part * sub, plane), LANES) if table_ref.shape[0] > 1 else 0
    copy = pltpu.make_async_copy(table_ref.at[variant], tables, sem)
    copy.start()

    for k, chunk in enumerate((c0, c1, c2, c3)):
        source = sub ^ k
        for half in range(2):
            base = pl.multiple_of((2 * source + half) * 32, 32)
            rows[pl.ds(base + 8, 16), :] = chunk[half * 16:half * 16 + 16, :]
            at = k * 16 + half * 8
            rows[pl.ds(pl.multiple_of(base + 24 * (1 - core), 8), 8), :] = inner_ref[at:at + 8, :]
            rows[pl.ds(pl.multiple_of(base + 24 * core, 8), 8), :] = outer_ref[at:at + 8, :]
    for place in range(1, COLUMNS):
        lanes = slice(place * LANES, (place + 1) * LANES)
        for at in range(0, 256, 32):
            rolled[at:at + 32, lanes] = pltpu.roll(rows[at:at + 32, lanes], 64, 1)
    for at in range(0, comps.shape[0], 24):
        comps[at:at + 8, :] = jnp.zeros((8, LANES), jnp.float32)
        comps[at + 16:at + 24, :] = jnp.zeros((8, LANES), jnp.float32)
    total[...] = jnp.zeros_like(total)

    def split_store(ref, at, place, values):
        high, low = split_bf16(values)
        for third, piece in enumerate((high, low, high)):
            lanes = third * 256 + place * LANES
            ref[pl.ds(at, 16), lanes:lanes + LANES] = piece

    def factors(block, piece):
        odd = (block >= half_blocks).astype(jnp.int32)
        owner = slab ^ (2 * ((block - half_blocks * odd) * piece_count + piece) + odd)
        freq_x = lax.div(freq_part * (sub_count * owner + sub), plane)
        return [factor_ref[freq_x, row:row + 1, :] for row in range(8)]

    pieces_in[...] = jnp.zeros_like(pieces_in)

    for group in range(class_count):
        for piece in range(piece_count):

            def transform_x(index, _):
                factor = factors(group * class_blocks + index, piece)
                for at in range(0, 256, 16):
                    def column(ref, place):
                        return ref[at:at + 16, place * LANES:(place + 1) * LANES]

                    full = column(rows, 0) + (factor[0] * column(rows, 1) + factor[1] * column(rolled, 1))
                    ring = None
                    for pair in range(3):
                        term = (
                            factor[2 + 2 * pair] * column(rows, 2 + pair)
                            + factor[3 + 2 * pair] * column(rolled, 2 + pair)
                        )
                        ring = term if ring is None else ring + term
                    target = pl.multiple_of(index * 256 + at, 16)
                    split_store(layers, target, 0, full)
                    split_store(layers, target, 1, ring)
                return 0

            lax.fori_loop(0, class_blocks, transform_x, 0)
            if group == 0 and piece == 0:
                copy.wait()
            found = jnp.dot(layers[...], tables[group * piece_count + piece, 0], preferred_element_type=jnp.float32)
            span = slice(group * class_blocks * 256, (group + 1) * class_blocks * 256)
            for part in range(2):
                values = found[:, part * LANES:(part + 1) * LANES]
                if piece > 0:
                    values = values + spectra[part, span, :]
                spectra[part, span, :] = values

    for block in range(block_count):
        for part in range(2):
            left = block_refs[block][pl.ds(part, KEPT, stride=2), :]
            lanes = slice(part * LANES, (part + 1) * LANES)
            for turn in range(3):
                piece = left.astype(jnp.bfloat16)
                left = left - piece.astype(jnp.float32)
                pieces_in[block % 2, turn * KEPT_PADDED:turn * KEPT_PADDED + KEPT, lanes] = piece
        result = jnp.dot(matrix_ref[...], pieces_in[block % 2], preferred_element_type=jnp.float32)
        k_re, k_im = result[:, :LANES], result[:, LANES:]
        for part, value in enumerate((k_re, k_im - k_re, k_re + k_im)):
            kernel_ref[block, part] = value

    def translate_block(block):
        for parent in range(4):
            values = np.empty((2, 3, 3, 3), dtype=object)
            for part in range(2):
                for px in range(2):
                    for py in range(2):
                        for pz in range(2):
                            row = block * 256 + (2 * parent + px) * 4 + pz * 2 + py
                            values[part, px, py, pz] = spectra[part, pl.ds(row, 8, stride=32), :]
                for px in range(2):
                    for py in range(2):
                        values[part, px, py, 2] = values[part, px, py, 0] + values[part, px, py, 1]
                    for cz in range(3):
                        values[part, px, 2, cz] = values[part, px, 0, cz] + values[part, px, 1, cz]
                for cy in range(3):
                    for cz in range(3):
                        values[part, 2, cy, cz] = values[part, 0, cy, cz] + values[part, 1, cy, cz]
            for comp in range(27):
                for part in range(2):
                    value = values[part, comp // 9, comp // 3 % 3, comp % 3]
                    at = ((comp * 4 + parent) * 2 + part) * 24 + 8
                    comps[at:at + 8, :] = value

        def product(cx, cy, cz):
            comp = (cx * 3 + cy) * 3 + cz
            have = [[None] * 3 for _ in range(2)]
            for ey in (-1, 0, 1):
                source = []
                for parent in range(4):
                    at = (comp * 4 + parent) * 48 + 8 + ey
                    s_re, s_im = (comps[at + 24 * part:at + 24 * part + 8, :] for part in range(2))
                    source.append((s_re + s_im, s_re, s_im))
                for place, (ex, neighbour_y) in enumerate(NEIGHBOURS):
                    if neighbour_y != ey:
                        continue
                    row = comp * 8 + place
                    weights = [
                        jnp.broadcast_to(kernel_ref[block, part, row:row + 1, :], (8, LANES)) for part in range(3)
                    ]
                    for parent in range(2):
                        for part in range(3):
                            term = weights[part] * source[parent + 1 + ex][part]
                            old = have[parent][part]
                            have[parent][part] = term if old is None else old + term
            found = []
            for parent in range(2):
                first, second, third = have[parent]
                found += [first - third, first + second]
            return found

        def merge(low, high, both):
            return [b + h for b, h in zip(both, high)] + [b + l for b, l in zip(both, low)]

        def along_z(cx, cy):
            return merge(product(cx, cy, 0), product(cx, cy, 1), product(cx, cy, 2))

        def along_y(cx):
            return merge(along_z(cx, 0), along_z(cx, 1), along_z(cx, 2))

        values = merge(along_y(0), along_y(1), along_y(2))
        for px in range(2):
            for py in range(2):
                for pz in range(2):
                    for parent in range(2):
                        at = ((px * 2 + py) * 2 + pz) * 4 + parent * 2
                        row = (2 * parent + px) * 4 + pz * 2 + py
                        for part in range(2):
                            sums[part, pl.ds(row, 8, stride=16), :] = values[at + part]
        for at in range(0, 128, 16):
            for part in range(2):
                split_store(split_sums, pl.multiple_of(block * 128 + at, 16), part, sums[part, at:at + 16, :])

    def one_block(block, _):
        translate_block(block)
        return 0

    lax.fori_loop(0, block_count, one_block, 0)

    for group in range(class_count):
        span = slice(group * class_blocks * 128, (group + 1) * class_blocks * 128)
        for piece in range(piece_count):
            moved[...] = jnp.dot(split_sums[span, :], tables[group * piece_count + piece, 1], preferred_element_type=jnp.float32)

            def transform_back(index, _):
                factor = factors(group * class_blocks + index, piece)
                for at in range(0, 128, 16):
                    source = pl.ds(pl.multiple_of(index * 128 + at, 16), 16)
                    full, ring = moved[source, :LANES], moved[source, LANES:]
                    full_rolled, ring_rolled = pltpu.roll(full, 64, 1), pltpu.roll(ring, 64, 1)
                    total[at:at + 16, 0:LANES] += full
                    total[at:at + 16, LANES:2 * LANES] += factor[0] * full - factor[1] * full_rolled
                    for pair in range(3):
                        lanes = slice((2 + pair) * LANES, (3 + pair) * LANES)
                        total[at:at + 16, lanes] += (
                            factor[2 + 2 * pair] * ring - factor[3 + 2 * pair] * ring_rolled
                        )
                return 0

            lax.fori_loop(0, class_blocks, transform_back, 0)

    for k, out_ref in enumerate((o0, o1, o2, o3)):
        base = pl.multiple_of((sub ^ k) * 32, 32)
        out_ref[...] = total[pl.ds(base, 32), :] * (1.0 / 4096.0)


def translate(sub_count, freq_part, chunks, inner, outer, tables, blocks):
    block_count = len(blocks)
    class_blocks = block_count * (LANES // freq_part) // tables.shape[1]
    width = COLUMNS * LANES
    matrix = jnp.asarray(np.concatenate([expansion()] * 3, axis=1), jnp.bfloat16)
    f32, bf16 = jnp.float32, jnp.bfloat16
    in_vmem = pl.BlockSpec(memory_space=pltpu.VMEM)
    anywhere = pl.BlockSpec(memory_space=pl.ANY)
    return pl.pallas_call(
        functools.partial(translate_body, sub_count, freq_part),
        in_specs=[in_vmem] * 8 + [anywhere] + [in_vmem] * block_count,
        out_specs=[in_vmem] * 4,
        scratch_shapes=[
            pltpu.VMEM((256, width), f32),
            pltpu.VMEM((256, width), f32),
            pltpu.VMEM((class_blocks * 256, 768), bf16),
            pltpu.VMEM((2, block_count * 256, LANES), f32),
            pltpu.VMEM((4 * 54 * 24, LANES), f32),
            pltpu.VMEM((2, 128, LANES), f32),
            pltpu.VMEM((block_count * 128, 768), bf16),
            pltpu.VMEM((class_blocks * 128, 256), f32),
            pltpu.VMEM((128, width), f32),
            pltpu.VMEM(tables.shape[1:], bf16),
            pltpu.VMEM((2, 3 * KEPT_PADDED, 2 * LANES), bf16),
            pltpu.VMEM((block_count, 3, 27 * 8, LANES), f32),
            pltpu.SemaphoreType.DMA,
        ],
        out_shape=[jax.ShapeDtypeStruct((32, width), f32)] * 4,
        compiler_params=pltpu.CompilerParams(vmem_limit_bytes=VMEM_BYTES),
        name="translate",
    )(*chunks, inner, outer, jnp.asarray(layer_factors()), matrix, tables, *blocks)


def plane_layout():
    points = surface_points(P_SIZE)
    layer = points[1:, points[0] == 1]
    at_y, at_z, used, part = (np.zeros(256, np.int32) for _ in range(4))
    at_y[:128], at_z[:128] = np.arange(128) % 64 // 8, np.arange(128) % 8
    used[:128], part[:128] = 1, np.arange(128) // 64
    for half in range(2):
        for slot in range(2):
            base = 128 + 64 * half + 32 * slot
            at_y[base:base + 28], at_z[base:base + 28] = layer
            used[base:base + 28], part[base:base + 28] = 1, half
    return at_y, at_z, used, part


def plane_tables(freq, freq_part):
    side = 2 * P_SIZE
    at_y, at_z, used, part = plane_layout()
    lib = np if isinstance(freq, np.ndarray) else jnp
    freq_y, freq_z = freq // side % side, freq % side
    column = lambda values: values[None, :, None]
    turns = column(at_y) * freq_y[:, None, :] + column(at_z) * freq_z[:, None, :]
    quarter = side // 4
    turns = lib.concatenate([turns - quarter * column(part), turns + quarter * column(1 - part)], axis=2)
    values = lib.cos((turns % side).astype(np.float32) * np.float32(2.0 * math.pi / side)) * column(used.astype(np.float32))
    pieces = LANES // freq_part
    owner = np.arange(2 * LANES) % LANES // freq_part
    mine = (owner[None, :] == np.arange(pieces)[:, None]).astype(np.float32)
    values = (values[:, None] * mine[None, :, None, :]).reshape(-1, 256, 256)
    if lib is np:
        high = values.astype(jnp.bfloat16).astype(np.float32)
    else:
        high = lax.reduce_precision(values, 8, 7)
    low = values - high
    both = []
    for turned in (False, True):
        third = [lib.swapaxes(piece, 1, 2) if turned else piece for piece in (high, high, low)]
        both.append(lib.concatenate(third, axis=1))
    return lib.stack(both, axis=1).astype(jnp.bfloat16)


def layer_factors():
    side = 2 * P_SIZE
    lane = np.arange(LANES)
    layer = np.stack([np.full(LANES, 7)] + [2 * pair + 1 + lane % 64 // 32 for pair in range(3)])
    sign = np.where(lane < 64, 1.0, -1.0)
    angles = (layer[None] * np.arange(side)[:, None, None] % side) * (2.0 * math.pi / side)
    both = np.stack([np.cos(angles), np.sin(angles) * sign], axis=2)
    return both.reshape(side, 8, LANES).astype(np.float32)


def local(density, occupied, kernels):
    block_x, block_y, block_z, surf_count = density.shape[1:]
    slab_count = lax.axis_size("slab")
    sub_count = lax.axis_size("sub")
    freq_part = kernels.shape[-1]
    assert (block_x, block_y, block_z, sub_count) == (4, 4, 2, 4)
    slab, sub = lax.axis_index("slab"), lax.axis_index("sub")
    core = slab % 2

    def exchange(values, axis, bits):
        pairs = [(i, i ^ bits) for i in range(lax.axis_size(axis))]
        return lax.ppermute(values, axis, pairs)

    own, mine = prepare(occupied, density, kernels)
    width = own.shape[-1]
    chunks = [own] + [exchange(own, "sub", k) for k in range(1, 4)]

    same_core = [mine] + [exchange(mine, "slab", m) for m in range(2, slab_count, 2)]

    def rows_at(start):
        parts = [lax.dynamic_slice_in_dim(chunk.reshape(2, 16, width), start, 8, 1) for chunk in chunks]
        return jnp.concatenate(parts).reshape(64, width)

    across = [(i, i + 1) for i in range(1, slab_count - 1, 2)]
    across += [(right, left) for left, right in across]
    outer, inner = rows_at(8 * core), rows_at(8 * (1 - core))
    sibling = exchange(mine, "slab", 1)
    _, _, same_core, sibling = lax.optimization_barrier((outer, inner, same_core, sibling))
    outer = lax.ppermute(outer, "slab", across)
    inner = exchange(inner, "slab", 1)

    other_core = [sibling] + [exchange(block, "slab", 1) for block in same_core[1:]]
    pieces = LANES // freq_part
    block_count = slab_count // pieces

    def by_block(blocks):
        return [jnp.concatenate(blocks[at:at + pieces], axis=1) for at in range(0, len(blocks), pieces)]

    blocks = same_core + other_core if pieces == 1 else by_block(same_core) + by_block(other_core)
    plane = 4 * P_SIZE * P_SIZE
    if pieces == 1 and (freq_part * sub_count) % plane == 0:
        freq = np.arange(plane, dtype=np.int32).reshape(-1, LANES)
        tables = jnp.asarray(plane_tables(freq, freq_part))[:, None]
    else:
        owner = slab ^ jnp.asarray([2 * k + half for half in range(2) for k in range(pieces)], jnp.int32)
        base = freq_part * (sub_count * owner + sub)
        freq = (base[:, None] + jnp.arange(freq_part)[None, :]).reshape(2, LANES).astype(jnp.int32)
        tables = plane_tables(freq, freq_part)[None]

    parts = translate(sub_count, freq_part, chunks, inner, outer, tables, blocks)
    fields = [parts[0]] + [exchange(parts[k], "sub", k) for k in (3, 2, 1)]
    return unpack(occupied, fields, density.shape)


def solution(mesh):
    return jax.shard_map(
        local,
        mesh=mesh,
        in_specs=(
            P(None, "slab", "sub", None, None),
            P("slab", "sub", None),
            P(None, None, ("slab", "sub")),
        ),
        out_specs=P(None, "slab", "sub", None, None),
        check_vma=False,
    )
```
